512 devices in a mesh: prow: 32 (over z, core), pcol: 16 (over x, y).
Axes of the slice: x: 4, y: 4, z: 16, core: 2. Of those that a mesh axis runs over, the one named last changes fastest.
Arguments:
- eigen_in: float32 [1536, 155648], P('pcol', 'prow'), may hold values from -6 to 6
- house_vecs: float32 [4, 128, 155648], P(None, 'pcol', 'prow'), may hold values from -6 to 6
- wy_factor: float32 [4, 128, 128], P(None, 'pcol'), as said below
Outputs:
- eigen_out: float32 [1536, 155648], P('pcol', 'prow')
The draws below stay inside these ranges and needn't reach their ends.
Inputs may be any that keep to these rules, and one draw needn't show every extreme that they name: `wy_factor`: each block's matrix is upper triangular.
All inputs are finite; a program needn't handle non-finite values.
Results may differ from the reference program's by a relative error of at most 0.00014.
Values sent between devices are 32-bit elements; how exact they have to be, the bound alone decides.
No kernel may reach another device: no remote copies, remote signals or barrier semaphores. Data moves between devices by JAX's collectives and lax.ppermute only.
A program may use at most 64 MiB of HBM per device.

```python
import math
import jax
import jax.numpy as jnp
from jax import lax

N = 155648
KB = 128
NBLK = 4
MEIG = 1536


def draw_wy_factor(key, part):
    key = jax.random.fold_in(key, 7)
    key_diag, key_upper = jax.random.split(key)
    diagonal = jax.random.uniform(key_diag, (NBLK, KB), jnp.float32, 1.0, 2.0)
    upper = jax.random.normal(key_upper, (NBLK, KB, KB), jnp.float32) * 0.5
    rows_idx = lax.broadcasted_iota(jnp.int32, (KB, KB), 0)
    cols_idx = lax.broadcasted_iota(jnp.int32, (KB, KB), 1)
    strict = (cols_idx > rows_idx).astype(jnp.float32)
    ident = (cols_idx == rows_idx).astype(jnp.float32)
    matrix = upper * strict / math.sqrt(KB) + diagonal[:, :, None] * ident
    return matrix / N


def block_levels(rng, dims, pieces, low, top_value):
    def one(axis_at, parts):
        heights = jax.random.uniform(jax.random.fold_in(jax.random.fold_in(rng, 6), axis_at), (parts,), jnp.float32, low / len(pieces), top_value / len(pieces))
        return jnp.repeat(jnp.exp(heights), dims[axis_at] // parts).reshape((-1,) + (1,) * (len(dims) - axis_at - 1))

    level = one(*pieces[0])
    for cut in pieces[1:]:
        level = level * one(*cut)
    return level


def gaussian(own_key, extent, deviation, most, cuts=(), kind=jnp.bfloat16):
    array = jax.random.normal(own_key, extent, jnp.float32) * deviation
    if len(cuts) > 0:
        array = block_levels(own_key, extent, cuts, -0.22, 0.18) * array
    return jnp.clip(array, min=-most, max=most).astype(kind)


def setup_inputs(seed: int = 0) -> dict:
    splits = jax.random.split(jax.random.key(seed), 4)
    eigen_in = gaussian(splits[0], (MEIG, N), 1.0, 6.0, ((0, 16), (1, 32)), jnp.float32)
    house_vecs = gaussian(splits[1], (NBLK, KB, N), 1.0, 6.0, ((1, 16), (2, 32)), jnp.float32)
    wy_factor = draw_wy_factor(jax.random.fold_in(splits[3], 71), 0)
    return dict(eigen_in=eigen_in, house_vecs=house_vecs, wy_factor=wy_factor)


def inner_rows(left, right):
    return lax.dot_general(left, right, (((1,), (1,)), ((), ())), precision=lax.Precision.HIGHEST, preferred_element_type=jnp.float32)


def plain_product(left, right):
    return jnp.dot(left, right, precision=lax.Precision.HIGHEST, preferred_element_type=jnp.float32)


def reference(eigen_in, house_vecs, wy_factor):
    current = eigen_in
    for block in range(NBLK):
        vectors = house_vecs[block]
        projection = inner_rows(current, vectors)
        scaled = inner_rows(projection, wy_factor[block])
        current = current - plain_product(scaled, vectors)
    return current
```

```python
import jax
import jax.numpy as jnp
from jax import lax
from jax.experimental import pallas as pl
from jax.experimental.pallas import tpu as pltpu
from jax.sharding import PartitionSpec as P

F32 = jnp.float32
BF16 = jnp.bfloat16
NT = (((1,), (1,)), ((), ()))
NN = (((1,), (0,)), ((), ()))


def split(x):
    high = x.astype(BF16)
    low = (x - high.astype(F32)).astype(BF16)
    return high, low


def product(left, right, dims):
    rows = left[0].shape[0]
    both = lax.dot_general(
        jnp.concatenate(left, axis=0), right[0], dims, preferred_element_type=F32
    )
    cross = lax.dot_general(left[0], right[1], dims, preferred_element_type=F32)
    return both[:rows] + (both[rows:] + cross)


def exact(left, right, dims):
    return lax.dot_general(
        left, right, dims, precision=lax.Precision.HIGHEST, preferred_element_type=F32
    )


def pair_list(nblk):
    return [(b, c) for b in range(nblk) for c in range(b + 1, nblk)]


def inner_kernel(half, core_ref, eig_ref, vec_ref, keep_ref, give_ref, high, low, total):
    rows = eig_ref.shape[0]
    owners, nblk, share, width = vec_ref.shape
    kb = owners * share
    step = pl.program_id(0)

    @pl.when(step == 0)
    def _():
        total[...] = jnp.zeros_like(total)

    high[:rows], low[:rows] = split(eig_ref[...])
    for b in range(nblk):
        at = rows + b * kb
        high[at : at + kb], low[at : at + kb] = split(vec_ref[:, b].reshape(kb, width))

    first_pair = nblk * rows
    pairs = pair_list(nblk)
    for c0 in range(0, nblk, 2):
        c1 = min(c0 + 2, nblk)
        top = rows + (c1 - 1) * kb
        cols = slice(rows + c0 * kb, rows + c1 * kb)
        out = product((high[:top], low[:top]), (high[cols], low[cols]), NT)
        for c in range(c0, c1):
            lane = slice((c - c0) * kb, (c - c0 + 1) * kb)
            total[c * rows : (c + 1) * rows] += out[:rows, lane]
            for b in range(c):
                at = first_pair + pairs.index((b, c)) * kb
                total[at : at + kb] += out[rows + b * kb : rows + (b + 1) * kb, lane]

    @pl.when(step == pl.num_programs(0) - 1)
    def _():
        core = core_ref[0]
        keep_ref[...] = total[pl.ds(pl.multiple_of(core * half, 8), half)]
        give_ref[...] = total[pl.ds(pl.multiple_of((1 - core) * half, 8), half)]


def inner_sums(core, eig, vecs, half):
    rows, cols = eig.shape
    owners, nblk, share, _ = vecs.shape
    kb = owners * share
    width = cols // 2
    depth = rows + nblk * kb
    return pl.pallas_call(
        lambda *refs: inner_kernel(half, *refs),
        out_shape=[jax.ShapeDtypeStruct((half, kb), F32)] * 2,
        grid_spec=pltpu.PrefetchScalarGridSpec(
            num_scalar_prefetch=1,
            grid=(2,),
            in_specs=[
                pl.BlockSpec((rows, width), lambda t, _: (0, t)),
                pl.BlockSpec((owners, nblk, share, width), lambda t, _: (0, 0, 0, t)),
            ],
            out_specs=[pl.BlockSpec((half, kb), lambda t, _: (0, 0))] * 2,
            scratch_shapes=[
                pltpu.VMEM((depth, width), BF16),
                pltpu.VMEM((depth, width), BF16),
                pltpu.VMEM((2 * half, kb), F32),
            ],
        ),
        compiler_params=pltpu.CompilerParams(vmem_limit_bytes=48 * 2**20),
        name="inner_sums",
    )(core, eig, vecs)


def update_kernel(sum_ref, fac_ref, eig_ref, vec_ref, out_ref, high, low):
    rows, width = eig_ref.shape
    owners, nblk, share, _ = vec_ref.shape
    kb = owners * share
    first_pair = nblk * rows
    pairs = pair_list(nblk)

    @pl.when(pl.program_id(0) == 0)
    def _():
        scaled = []
        for c in range(nblk):
            proj = sum_ref[c * rows : (c + 1) * rows]
            for b in range(c):
                at = first_pair + pairs.index((b, c)) * kb
                proj = proj - exact(scaled[b], sum_ref[at : at + kb], NN)
            scaled.append(exact(proj, fac_ref[:, c].reshape(kb, kb), NT))
            lane = slice(c * kb, (c + 1) * kb)
            high[:, lane], low[:, lane] = split(scaled[c])

    left = (high[...], low[...])
    for at in range(0, width, 256):
        lane = slice(at, min(at + 256, width))
        vecs = jnp.concatenate(
            [vec_ref[:, b, :, lane].reshape(kb, lane.stop - at) for b in range(nblk)], axis=0
        )
        out_ref[:, lane] = eig_ref[:, lane] - product(left, split(vecs), NN)


def update(sums, factors, eig, vecs):
    rows, cols = eig.shape
    owners, nblk, share, _ = vecs.shape
    kb = owners * share
    width = cols // 2
    return pl.pallas_call(
        update_kernel,
        out_shape=jax.ShapeDtypeStruct(eig.shape, F32),
        grid=(2,),
        in_specs=[
            pl.BlockSpec(sums.shape, lambda t: (0, 0)),
            pl.BlockSpec(factors.shape, lambda t: (0, 0, 0, 0)),
            pl.BlockSpec((rows, width), lambda t: (0, t)),
            pl.BlockSpec((owners, nblk, share, width), lambda t: (0, 0, 0, t)),
        ],
        out_specs=pl.BlockSpec((rows, width), lambda t: (0, t)),
        scratch_shapes=[pltpu.VMEM((rows, nblk * kb), BF16)] * 2,
        compiler_params=pltpu.CompilerParams(vmem_limit_bytes=48 * 2**20),
        name="update",
    )(sums, factors, eig, vecs)


def sum_over_rows(keep, give, nprow):
    half, kb = keep.shape
    nz = nprow // 2
    along_z = [list(range(core, nprow, 2)) for core in range(2)]
    in_chip = [[2 * z, 2 * z + 1] for z in range(nz)]
    mine = keep + lax.ppermute(give, "prow", [(i, i ^ 1) for i in range(nprow)])
    parts = lax.all_to_all(
        mine.reshape(nz, half // nz, kb), "prow", 0, 0, axis_index_groups=along_z
    )
    part = jnp.sum(parts, axis=0)
    whole = lax.all_to_all(
        jnp.broadcast_to(part, (nz,) + part.shape), "prow", 0, 0, axis_index_groups=along_z
    )
    return lax.all_gather(
        whole.reshape(half, kb), "prow", axis=0, tiled=True, axis_index_groups=in_chip
    )


def solution(mesh):
    placed = (P("pcol", "prow"), P(None, "pcol", "prow"), P(None, "pcol", None))
    nprow = mesh.shape["prow"]

    def per_device(eig, house_vecs, wy_factor):
        nblk, _, kb = wy_factor.shape
        vecs = lax.all_gather(house_vecs, "pcol", axis=0)
        factors = lax.all_gather(wy_factor, "pcol", axis=0)
        filled = nblk * eig.shape[0] + len(pair_list(nblk)) * kb
        half = -(-filled // (8 * nprow)) * 8 * nprow // 2
        core = lax.rem(lax.axis_index("prow"), 2).astype(jnp.int32).reshape(1)
        keep, give = inner_sums(core, eig, vecs, half)
        sums = sum_over_rows(keep, give, nprow)
        return update(sums, factors, eig, vecs)

    return jax.shard_map(
        per_device, mesh=mesh, in_specs=placed, out_specs=P("pcol", "prow"), check_vma=False
    )
```

```python
import jax
import jax.numpy as jnp
import numpy as np
from jax import lax
from jax.experimental import pallas as pl
from jax.experimental.pallas import tpu as pltpu
from jax.sharding import PartitionSpec as P

F32 = jnp.float32
BF16 = jnp.bfloat16
NT = (((1,), (1,)), ((), ()))
NN = (((1,), (0,)), ((), ()))
VMEM_LIMIT = 52 * 2**20
X_NEAR, X_WRAP, Y_NEAR, Y_WRAP = 4, 12, 1, 3
ROUTES = (
    ((X_NEAR, X_WRAP, Y_NEAR, Y_WRAP), (Y_NEAR, Y_WRAP, X_NEAR, X_WRAP)),
    ((X_WRAP, X_NEAR, Y_WRAP, Y_NEAR), (Y_WRAP, Y_NEAR, X_WRAP, X_NEAR)),
)


def split(x):
    high = x.astype(BF16)
    low = (x - high.astype(F32)).astype(BF16)
    return high, low


def product(left, right, dims):
    rows = left[0].shape[0]
    both = lax.dot_general(
        jnp.concatenate(left, axis=0), right[0], dims, preferred_element_type=F32
    )
    cross = lax.dot_general(left[0], right[1], dims, preferred_element_type=F32)
    return both[:rows] + (both[rows:] + cross)


def exact(left, right, dims):
    return lax.dot_general(
        left, right, dims, precision=lax.Precision.HIGHEST, preferred_element_type=F32
    )


def pair_list(nblk):
    return [(b, c) for b in range(nblk) for c in range(b + 1, nblk)]


def chunks_of(width):
    first = -(-width // 512) * 256
    return [(0, first), (first, width - first)]


def arrival_order(route):
    order = [0]
    for mask in route:
        order = order + [mask ^ at for at in order]
    return order


def gather_copies(order_ref, part, bufs, into, lane, sems):
    copies = []
    for k, buf in enumerate(bufs):
        for i in range(buf.shape[0]):
            slot = k * buf.shape[0] + i
            owner = order_ref[part, slot]
            copies.append(
                pltpu.make_async_copy(
                    buf.at[i, :, :, lane], into.at[owner, :, :, lane], sems.at[slot]
                )
            )
    return copies


def inner_kernel(part, half, order_ref, core_ref, *refs):
    last = part == 1
    eig_ref, bufs, refs = refs[0], refs[1:5], refs[5:]
    if last:
        before_ref, refs = refs[0], refs[1:]
    outs, refs = refs[: 1 + last], refs[1 + last :]
    vecs, eig, high, low, total, sems, eig_sems = refs
    rows = eig.shape[0]
    owners, nblk, share, _ = vecs.shape
    kb = owners * share
    width = eig.shape[1]
    start = eig_ref.shape[1] - width if last else 0
    pieces = chunks_of(width)

    copies = []
    for n, (at, size) in enumerate(pieces):
        lane = pl.ds(at, size)
        copies.append(
            gather_copies(order_ref, part, bufs, vecs, lane, sems.at[n])
            + [
                pltpu.make_async_copy(
                    eig_ref.at[:, pl.ds(start + at, size)], eig.at[:, lane], eig_sems.at[n]
                )
            ]
        )
        for copy in copies[n]:
            copy.start()
    total[...] = before_ref[...] if last else jnp.zeros_like(total)

    first_pair = nblk * rows
    pairs = pair_list(nblk)
    for n, (at, size) in enumerate(pieces):
        for copy in copies[n]:
            copy.wait()
        lane = slice(at, at + size)
        high[:rows, lane], low[:rows, lane] = split(eig[:, lane])
        for b in range(nblk):
            here = slice(rows + b * kb, rows + (b + 1) * kb)
            high[here, lane], low[here, lane] = split(vecs[:, b, :, lane].reshape(kb, size))
        for c0 in range(0, nblk, 2):
            c1 = min(c0 + 2, nblk)
            top = rows + (c1 - 1) * kb
            cols = slice(rows + c0 * kb, rows + c1 * kb)
            out = product(
                (high[:top, lane], low[:top, lane]), (high[cols, lane], low[cols, lane]), NT
            )
            for c in range(c0, c1):
                here = slice((c - c0) * kb, (c - c0 + 1) * kb)
                total[c * rows : (c + 1) * rows] += out[:rows, here]
                for b in range(c):
                    to = first_pair + pairs.index((b, c)) * kb
                    total[to : to + kb] += out[rows + b * kb : rows + (b + 1) * kb, here]

    if last:
        core = core_ref[0]
        outs[0][...] = total[pl.ds(pl.multiple_of(core * half, 8), half)]
        outs[1][...] = total[pl.ds(pl.multiple_of((1 - core) * half, 8), half)]
    else:
        outs[0][...] = total[...]


def inner_sums(part, half, order, core, eig, bufs, width, before=None):
    rows, cols = eig.shape
    _, nblk, share, buf_width = bufs[0].shape
    owners = sum(buf.shape[0] for buf in bufs)
    kb = owners * share
    depth = rows + nblk * kb
    last = part == 1
    vmem = pl.BlockSpec(memory_space=pltpu.VMEM)
    smem = pl.BlockSpec(memory_space=pltpu.SMEM)
    hbm = pl.BlockSpec(memory_space=pl.ANY)
    if last:
        outs = [jax.ShapeDtypeStruct((half, kb), F32)] * 2
    else:
        outs = [jax.ShapeDtypeStruct((2 * half, kb), F32)]
    products = width * kb * (nblk * rows + len(pair_list(nblk)) * kb)
    return pl.pallas_call(
        lambda *refs: inner_kernel(part, half, *refs),
        out_shape=outs,
        in_specs=[smem, smem] + [hbm] * 5 + [vmem] * last,
        out_specs=[vmem] * len(outs),
        scratch_shapes=[
            pltpu.VMEM((owners, nblk, share, width), F32),
            pltpu.VMEM((rows, width), F32),
            pltpu.VMEM((depth, width), BF16),
            pltpu.VMEM((depth, width), BF16),
            pltpu.VMEM((2 * half, kb), F32),
            pltpu.SemaphoreType.DMA((2, owners)),
            pltpu.SemaphoreType.DMA((2,)),
        ],
        compiler_params=pltpu.CompilerParams(vmem_limit_bytes=VMEM_LIMIT),
        cost_estimate=pl.CostEstimate(
            flops=6 * products, bytes_accessed=4 * width * depth, transcendentals=0
        ),
        name="inner_sums",
    )(order, core, eig, *bufs, *([before] if last else []))


def update_kernel(order_ref, sum_ref, eig_ref, *refs):
    bufs = (refs[0:4], refs[4:8])
    out_ref, vecs, eig, out, high, low = refs[8], refs[9:11], *refs[11:15]
    sems, eig_sems, out_sems = refs[15:]
    rows, cols = eig.shape
    owners, nblk, share, _ = vecs[0].shape
    kb = owners * share
    first_pair = nblk * rows
    pairs = pair_list(nblk)
    width_b = vecs[1].shape[3]
    width_a = cols - width_b

    eig_copies = []
    copies = []
    for part, (at, width) in enumerate(((0, width_a), (width_a, width_b))):
        whole = pl.ds(0, vecs[part].shape[3])
        copies.append(
            gather_copies(order_ref, part, bufs[part], vecs[part], whole, sems.at[part])
        )
        lane = pl.ds(at, width)
        eig_copies.append(
            pltpu.make_async_copy(eig_ref.at[:, lane], eig.at[:, lane], eig_sems.at[part])
        )
        for copy in copies[part]:
            copy.start()
        eig_copies[part].start()

    for copy in copies[0]:
        copy.wait()
    scaled = []
    for c in range(nblk):
        proj = sum_ref[c * rows : (c + 1) * rows]
        for b in range(c):
            at = first_pair + pairs.index((b, c)) * kb
            proj = proj - exact(scaled[b], sum_ref[at : at + kb], NN)
        factor = vecs[0][:, c, :, width_a : width_a + kb].reshape(kb, kb)
        scaled.append(exact(proj, factor, NT))
        lane = slice(c * kb, (c + 1) * kb)
        high[:, lane], low[:, lane] = split(scaled[c])

    left = (high[...], low[...])
    out_copies = []
    for part, (start, width) in enumerate(((0, width_a), (width_a, width_b))):
        if part > 0:
            for copy in copies[part]:
                copy.wait()
        eig_copies[part].wait()
        for at in range(0, width, 256):
            size = min(256, width - at)
            here = slice(start + at, start + at + size)
            right = jnp.concatenate(
                [vecs[part][:, b, :, at : at + size].reshape(kb, size) for b in range(nblk)],
                axis=0,
            )
            out[:, here] = eig[:, here] - product(left, split(right), NN)
        lane = pl.ds(start, width)
        out_copies.append(
            pltpu.make_async_copy(out.at[:, lane], out_ref.at[:, lane], out_sems.at[part])
        )
        out_copies[part].start()
    for copy in out_copies:
        copy.wait()


def update(order, sums, eig, parts):
    rows, cols = eig.shape
    _, nblk, share, _ = parts[0][0].shape
    owners = sum(buf.shape[0] for buf in parts[0])
    kb = owners * share
    vmem = pl.BlockSpec(memory_space=pltpu.VMEM)
    smem = pl.BlockSpec(memory_space=pltpu.SMEM)
    hbm = pl.BlockSpec(memory_space=pl.ANY)
    return pl.pallas_call(
        update_kernel,
        out_shape=jax.ShapeDtypeStruct(eig.shape, F32),
        in_specs=[smem, vmem] + [hbm] * 9,
        out_specs=hbm,
        scratch_shapes=[
            pltpu.VMEM((owners, nblk, share, parts[0][0].shape[3]), F32),
            pltpu.VMEM((owners, nblk, share, parts[1][0].shape[3]), F32),
            pltpu.VMEM((rows, cols), F32),
            pltpu.VMEM((rows, cols), F32),
            pltpu.VMEM((rows, nblk * kb), BF16),
            pltpu.VMEM((rows, nblk * kb), BF16),
            pltpu.SemaphoreType.DMA((2, owners)),
            pltpu.SemaphoreType.DMA((2,)),
            pltpu.SemaphoreType.DMA((2,)),
        ],
        compiler_params=pltpu.CompilerParams(vmem_limit_bytes=VMEM_LIMIT),
        cost_estimate=pl.CostEstimate(
            flops=6 * rows * nblk * kb * cols,
            bytes_accessed=4 * cols * (2 * rows + nblk * kb),
            transcendentals=0,
        ),
        name="update",
    )(order, sums, eig, *parts[0], *parts[1])


def gather_in_plane(own, part, nprow, npcol):
    def send(x, step):
        pairs = []
        for row in range(nprow):
            mask = ROUTES[part][row % 2][step]
            pairs += [(row * npcol + at, row * npcol + (at ^ mask)) for at in range(npcol)]
        return lax.ppermute(x, ("prow", "pcol"), pairs)

    held = own[None]
    held = jnp.concatenate([held, send(held, 0)], axis=0)
    held = jnp.concatenate([held, send(held, 1)], axis=0)
    third = send(held, 2)
    return held, third, send(held, 3), send(third, 3)


def sum_over_rows(keep, give, nprow):
    half, kb = keep.shape
    nz = nprow // 2
    along_z = [list(range(core, nprow, 2)) for core in range(2)]
    in_chip = [[2 * z, 2 * z + 1] for z in range(nz)]
    mine = keep + lax.ppermute(give, "prow", [(i, i ^ 1) for i in range(nprow)])
    parts = lax.all_to_all(
        mine.reshape(nz, half // nz, kb), "prow", 0, 0, axis_index_groups=along_z
    )
    part = jnp.sum(parts, axis=0)
    whole = lax.all_to_all(
        jnp.broadcast_to(part, (nz,) + part.shape), "prow", 0, 0, axis_index_groups=along_z
    )
    return lax.all_gather(
        whole.reshape(half, kb), "prow", axis=0, tiled=True, axis_index_groups=in_chip
    )


def solution(mesh):
    placed = (P("pcol", "prow"), P(None, "pcol", "prow"), P(None, "pcol", None))
    nprow, npcol = mesh.shape["prow"], mesh.shape["pcol"]
    orders = np.array([[arrival_order(route) for route in routes] for routes in ROUTES], np.int32)

    def per_device(eig, house_vecs, wy_factor):
        nblk, _, kb = wy_factor.shape
        rows, cols = eig.shape
        width_a = (cols // 128 - 1) // 2 * 128
        core = lax.rem(lax.axis_index("prow"), 2).astype(jnp.int32)
        order = jnp.bitwise_xor(
            lax.axis_index("pcol").astype(jnp.int32),
            jnp.where(core == 0, orders[:, 0], orders[:, 1]),
        )
        own_a = jnp.concatenate([house_vecs[:, :, :width_a], wy_factor], axis=2)
        own_b = house_vecs[:, :, width_a:]
        part_a = gather_in_plane(own_a, 0, nprow, npcol)
        part_b = gather_in_plane(own_b, 1, nprow, npcol)
        filled = nblk * rows + len(pair_list(nblk)) * kb
        half = -(-filled // (8 * nprow)) * 8 * nprow // 2
        core = core.reshape(1)
        (before,) = inner_sums(0, half, order, core, eig, part_a, width_a)
        keep, give = inner_sums(1, half, order, core, eig, part_b, cols - width_a, before)
        sums = sum_over_rows(keep, give, nprow)
        return update(order, sums, eig, (part_a, part_b))

    return jax.shard_map(
        per_device, mesh=mesh, in_specs=placed, out_specs=P("pcol", "prow"), check_vma=False
    )
```

```python
import jax
import jax.numpy as jnp
import numpy as np
from jax import lax
from jax.experimental import pallas as pl
from jax.experimental.pallas import tpu as pltpu
from jax.sharding import PartitionSpec as P

F32 = jnp.float32
BF16 = jnp.bfloat16
NT = (((1,), (1,)), ((), ()))
NN = (((1,), (0,)), ((), ()))
VMEM_LIMIT = 52 * 2**20
X_NEAR, X_WRAP, Y_NEAR, Y_WRAP = 4, 12, 1, 3
PARTNER = (Y_WRAP, X_WRAP)
ROUTES = (
    ((Y_NEAR, X_NEAR, X_WRAP), (X_NEAR, Y_NEAR, Y_WRAP)),
    ((X_WRAP, Y_NEAR, X_NEAR), (Y_WRAP, X_NEAR, Y_NEAR)),
)
LATE_ROUTE = ((Y_NEAR, X_WRAP, X_NEAR), (X_NEAR, Y_WRAP, Y_NEAR))


def split(x):
    high = x.astype(BF16)
    low = (x - high.astype(F32)).astype(BF16)
    return high, low


def product(left, right, dims):
    def dot(x, y):
        return lax.dot_general(x, y, dims, preferred_element_type=F32)

    return dot(left[0], right[0]) + (dot(left[1], right[0]) + dot(left[0], right[1]))


def exact(left, right, dims):
    return lax.dot_general(
        left, right, dims, precision=lax.Precision.HIGHEST, preferred_element_type=F32
    )


def pair_list(nblk):
    return [(b, c) for b in range(nblk) for c in range(b + 1, nblk)]


def arrival_order(part, core):
    near, second, third = ROUTES[part][core]
    first = [0, near, PARTNER[core], PARTNER[core] ^ near]
    return [at ^ mask for mask in (0, second, third, second ^ third) for at in first]


def late_orders(core):
    near, second, third = LATE_ROUTE[core]
    group = [at ^ mask for mask in (0, second, third, second ^ third) for at in (0, near)]
    rows = [group]
    for part in range(2):
        near, second, third = ROUTES[part][core]
        rows.append(
            [
                PARTNER[core] ^ at ^ mask
                for mask in (0, second, third, second ^ third)
                for at in (0, near)
            ]
        )
    return rows


def owner_copies(order_ref, part, bufs, into, start, sems):
    copies = []
    slot = 0
    for buf in bufs:
        for i in range(buf.shape[0]):
            lane = pl.ds(start, buf.shape[3])
            copies.append(
                pltpu.make_async_copy(
                    buf.at[i], into.at[order_ref[part, slot], :, :, lane], sems.at[part, slot]
                )
            )
            slot += 1
    return copies


def inner_kernel(order_ref, info_ref, eig_ref, mate_ref, *refs):
    bufs = (refs[0:4], refs[4:8])
    keep_ref, give_ref, fac_ref = refs[8:11]
    vecs, eig, mate, high, low, gram, sems, eig_sems, mate_sems = refs[11:]
    rows, half = eig.shape
    owners, nblk, share, _ = vecs.shape
    kb = owners * share
    side, parity = info_ref[0], info_ref[1]
    width_a = bufs[0][0].shape[3]
    data_a = half - bufs[1][0].shape[3]
    pieces = ((0, 0, data_a), (width_a, data_a, half - data_a))

    copies = []
    for part, (start, at, size) in enumerate(pieces):
        lane = pl.ds(at, size)
        off = pl.multiple_of(side * half + at, 128)
        copies.append(
            owner_copies(order_ref, part, bufs[part], vecs, start, sems)
            + [
                pltpu.make_async_copy(
                    eig_ref.at[:, pl.ds(off, size)], eig.at[:, lane], eig_sems.at[part]
                ),
                pltpu.make_async_copy(
                    mate_ref.at[:, lane], mate.at[:, lane], mate_sems.at[part]
                ),
            ]
        )
        for copy in copies[part]:
            copy.start()

    pairs = pair_list(nblk)
    first = 2 * rows
    for part, (start, at, size) in enumerate(pieces):
        for copy in copies[part]:
            copy.wait()
        lane = slice(at, at + size)
        high[:rows, lane], low[:rows, lane] = split(eig[:, lane])
        high[rows:first, lane], low[rows:first, lane] = split(mate[:, lane])
        for b in range(nblk):
            here = slice(first + b * kb, first + (b + 1) * kb)
            high[here, lane], low[here, lane] = split(
                vecs[:, b, :, start : start + size].reshape(kb, size)
            )
        for c0 in range(0, nblk, 2):
            c1 = min(c0 + 2, nblk)
            top = first + (c1 - 1) * kb
            cols = slice(first + c0 * kb, first + c1 * kb)
            out = product(
                (high[:top, lane], low[:top, lane]), (high[cols, lane], low[cols, lane]), NT
            )
            for c in range(c0, c1):
                here = slice((c - c0) * kb, (c - c0 + 1) * kb)
                to = slice(c * rows, (c + 1) * rows)
                terms = [(keep_ref, to, out[:rows, here]), (give_ref, to, out[rows:first, here])]
                for b in range(c):
                    at_pair = pairs.index((b, c)) * kb
                    from_row = first + b * kb
                    terms.append(
                        (gram, slice(at_pair, at_pair + kb), out[from_row : from_row + kb, here])
                    )
                for ref, to, term in terms:
                    ref[to] = term if part == 0 else ref[to] + term

    for b in range(nblk):
        fac_ref[b] = vecs[:, b, :, data_a:width_a].reshape(kb, kb)
    below = nblk * rows
    count = gram.shape[0] // 2
    keep_ref[below:] = gram[pl.ds(pl.multiple_of(parity * count, 8), count)]
    give_ref[below:] = gram[pl.ds(pl.multiple_of((1 - parity) * count, 8), count)]


def inner_sums(order, info, eig, mate, parts):
    rows, half = mate.shape
    _, nblk, share, _ = parts[0][0].shape
    owners = order.shape[1]
    kb = owners * share
    width = parts[0][0].shape[3] + parts[1][0].shape[3]
    depth = 2 * rows + nblk * kb
    npair = len(pair_list(nblk))
    vmem = pl.BlockSpec(memory_space=pltpu.VMEM)
    smem = pl.BlockSpec(memory_space=pltpu.SMEM)
    hbm = pl.BlockSpec(memory_space=pl.ANY)
    out = jax.ShapeDtypeStruct((nblk * rows + npair // 2 * kb, kb), F32)
    return pl.pallas_call(
        inner_kernel,
        out_shape=[out, out, jax.ShapeDtypeStruct((nblk, kb, kb), F32)],
        in_specs=[smem, smem] + [hbm] * 10,
        out_specs=[vmem] * 3,
        scratch_shapes=[
            pltpu.VMEM((owners, nblk, share, width), F32),
            pltpu.VMEM((rows, half), F32),
            pltpu.VMEM((rows, half), F32),
            pltpu.VMEM((depth, half), BF16),
            pltpu.VMEM((depth, half), BF16),
            pltpu.VMEM((npair * kb, kb), F32),
            pltpu.SemaphoreType.DMA((2, owners)),
            pltpu.SemaphoreType.DMA((2,)),
            pltpu.SemaphoreType.DMA((2,)),
        ],
        compiler_params=pltpu.CompilerParams(vmem_limit_bytes=VMEM_LIMIT),
        cost_estimate=pl.CostEstimate(
            flops=6 * half * kb * (2 * nblk * rows + npair * kb),
            bytes_accessed=4 * half * depth,
            transcendentals=0,
        ),
        name="inner_sums",
    )(order, info, eig, mate, *parts[0], *parts[1])


def update_kernel(order_ref, late_ref, info_ref, sum_ref, rest_ref, fac_ref, eig_ref, *refs):
    near, group, far, refs = (refs[0:4], refs[4:8]), refs[8:12], (refs[12:14], refs[14:16]), refs[16:]
    out_ref, vecs, eig, out, gram, high, low = refs[0], refs[1:3], *refs[3:8]
    near_sems, late_sems, eig_sems, out_sems = refs[8:]
    rows, cols = eig.shape
    owners, nblk, share, _ = vecs[0].shape
    kb = owners * share
    half = cols // 2
    width_a = near[0][0].shape[3]
    data_a = half - near[1][0].shape[3]
    side, parity = info_ref[0], info_ref[1]
    offsets = [pl.multiple_of(side * half, 128), pl.multiple_of((1 - side) * half, 128)]
    lanes = [pl.ds(0, half), pl.ds(half, half)]

    copies = [[], owner_copies(late_ref, 0, group, vecs[1], 0, late_sems)]
    for part, start in enumerate((0, width_a)):
        copies[0] += owner_copies(order_ref, part, near[part], vecs[0], start, near_sems)
        copies[1] += owner_copies(late_ref, 1 + part, far[part], vecs[1], start, late_sems)
    eig_copies, out_copies = [], []
    for n in range(2):
        theirs = pl.ds(offsets[n], half)
        eig_copies.append(
            pltpu.make_async_copy(eig_ref.at[:, theirs], eig.at[:, lanes[n]], eig_sems.at[n])
        )
        out_copies.append(
            pltpu.make_async_copy(out.at[:, lanes[n]], out_ref.at[:, theirs], out_sems.at[n])
        )
        for copy in copies[n]:
            copy.start()
        eig_copies[n].start()

    below = nblk * rows
    count = gram.shape[0] // 2
    gram[pl.ds(pl.multiple_of(parity * count, 8), count)] = sum_ref[below:]
    gram[pl.ds(pl.multiple_of((1 - parity) * count, 8), count)] = rest_ref[...]
    pairs = pair_list(nblk)
    scaled = []
    for c in range(nblk):
        proj = sum_ref[c * rows : (c + 1) * rows]
        for b in range(c):
            at = pairs.index((b, c)) * kb
            proj = proj - exact(scaled[b], gram[at : at + kb], NN)
        scaled.append(exact(proj, fac_ref[c], NT))
        lane = slice(c * kb, (c + 1) * kb)
        high[:, lane], low[:, lane] = split(scaled[c])

    left = (high[...], low[...])
    for n in range(2):
        for copy in copies[n]:
            copy.wait()
        eig_copies[n].wait()
        for start, at, stop in ((0, 0, data_a), (width_a, data_a, half)):
            for one in range(at, stop, 256):
                size = min(256, stop - one)
                here = slice(n * half + one, n * half + one + size)
                there = slice(start + one - at, start + one - at + size)
                right = jnp.concatenate(
                    [vecs[n][:, b, :, there].reshape(kb, size) for b in range(nblk)], axis=0
                )
                out[:, here] = eig[:, here] - product(left, split(right), NN)
        out_copies[n].start()
    for copy in out_copies:
        copy.wait()


def update(order, late, info, sums, rest, factors, eig, near, group, far):
    rows, cols = eig.shape
    _, nblk, share, _ = near[0][0].shape
    owners = order.shape[1]
    kb = owners * share
    width = near[0][0].shape[3] + near[1][0].shape[3]
    vmem = pl.BlockSpec(memory_space=pltpu.VMEM)
    smem = pl.BlockSpec(memory_space=pltpu.SMEM)
    hbm = pl.BlockSpec(memory_space=pl.ANY)
    return pl.pallas_call(
        update_kernel,
        out_shape=jax.ShapeDtypeStruct(eig.shape, F32),
        in_specs=[smem] * 3 + [vmem] * 3 + [hbm] * 17,
        out_specs=hbm,
        scratch_shapes=[
            pltpu.VMEM((owners, nblk, share, width), F32),
            pltpu.VMEM((owners, nblk, share, width), F32),
            pltpu.VMEM((rows, cols), F32),
            pltpu.VMEM((rows, cols), F32),
            pltpu.VMEM((2 * rest.shape[0], kb), F32),
            pltpu.VMEM((rows, nblk * kb), BF16),
            pltpu.VMEM((rows, nblk * kb), BF16),
            pltpu.SemaphoreType.DMA((2, owners)),
            pltpu.SemaphoreType.DMA((3, owners // 2)),
            pltpu.SemaphoreType.DMA((2,)),
            pltpu.SemaphoreType.DMA((2,)),
        ],
        compiler_params=pltpu.CompilerParams(vmem_limit_bytes=VMEM_LIMIT),
        cost_estimate=pl.CostEstimate(
            flops=6 * rows * nblk * kb * cols,
            bytes_accessed=4 * cols * (2 * rows + nblk * kb),
            transcendentals=0,
        ),
        name="update",
    )(order, late, info, sums, rest, factors, eig, *near[0], *near[1], *group, *far[0], *far[1])


def solution(mesh):
    placed = (P("pcol", "prow"), P(None, "pcol", "prow"), P(None, "pcol", None))
    nprow, npcol = mesh.shape["prow"], mesh.shape["pcol"]
    orders = np.array(
        [[arrival_order(part, core) for core in range(2)] for part in range(2)], np.int32
    )
    lates = np.zeros((2, 3, npcol), np.int32)
    lates[:, :, : npcol // 2] = [late_orders(core) for core in range(2)]
    in_chip = [[2 * z, 2 * z + 1] for z in range(nprow // 2)]

    def send(x, masks):
        pairs = []
        for row in range(nprow):
            mask = masks[row % 2]
            pairs += [(row * npcol + at, row * npcol + (at ^ mask)) for at in range(npcol)]
        return lax.ppermute(x, ("prow", "pcol"), pairs)

    def after(x, *others):
        return lax.optimization_barrier((x,) + others)[0]

    def doubling(own, mates, part):
        steps = [(ROUTES[part][0][n], ROUTES[part][1][n]) for n in range(3)]
        first = jnp.stack([own, send(own, steps[0]), mates, send(mates, steps[0])])
        second = send(first, steps[1])
        return first, second, send(first, steps[2]), steps[2]

    def along_z(x):
        nz = nprow // 2
        groups = [list(range(core, nprow, 2)) for core in range(2)]
        return lax.all_to_all(x, "prow", 0, 0, axis_index_groups=groups)

    def per_device(eig, house_vecs, wy_factor):
        nblk, _, kb = wy_factor.shape
        rows, cols = eig.shape
        half = cols // 2
        data_a = (half // 128 - 1) // 2 * 128
        width_a = data_a + kb
        at = lax.axis_index("pcol").astype(jnp.int32)
        core = lax.rem(lax.axis_index("prow"), 2).astype(jnp.int32)
        side = jnp.bitwise_and(jnp.where(core == 0, at >> 1, at >> 3), 1)
        parity = jnp.bitwise_and(jnp.bitwise_xor(at >> 1, at >> 3), 1)
        info = jnp.stack([side, parity])
        order = jnp.bitwise_xor(at, jnp.where(core == 0, orders[:, 0], orders[:, 1]))
        late = jnp.bitwise_xor(at, jnp.where(core == 0, lates[0], lates[1]))

        def columns(x, which):
            return lax.dynamic_slice_in_dim(x, which * half, half, axis=x.ndim - 1)

        vec_other = columns(house_vecs, 1 - side)
        vec_other = jnp.concatenate(
            [vec_other[:, :, :data_a], wy_factor, vec_other[:, :, data_a:]], axis=2
        )
        mates = send(vec_other, PARTNER)
        vec_mine = columns(house_vecs, side)
        own_a = jnp.concatenate([vec_mine[:, :, :data_a], wy_factor], axis=2)
        own_b = vec_mine[:, :, data_a:]
        near_a = doubling(own_a, mates[:, :, :width_a], 0)
        near_b = doubling(own_b, mates[:, :, width_a:], 1)
        eig_other = after(columns(eig, 1 - side), mates)
        mate_eig = send(eig_other, PARTNER)
        near = tuple(
            (first, second, third, send(after(second, mate_eig), step))
            for first, second, third, step in (near_a, near_b)
        )
        keep, give, factors = inner_sums(order, info, eig, mate_eig, near)

        late_steps = [(LATE_ROUTE[0][n], LATE_ROUTE[1][n]) for n in range(3)]
        own = after(vec_other, keep)[None]
        one = send(own, late_steps[0])
        sums = keep + send(give, PARTNER)
        pair = jnp.concatenate([own, one])
        pair = after(pair, sums)
        two = send(pair, late_steps[1])
        three = send(pair, late_steps[2])
        early = [
            send(after(jnp.concatenate([part[0][:2], part[1][:2]]), sums), PARTNER) for part in near
        ]
        count = sums.shape[0] // 2
        mine = lax.dynamic_slice_in_dim(sums, core * count, count)
        theirs = lax.dynamic_slice_in_dim(sums, (1 - core) * count, count)
        mine = mine + lax.ppermute(theirs, "prow", [(i, i ^ 1) for i in range(nprow)])
        nz = nprow // 2
        part = jnp.sum(along_z(mine.reshape(nz, count // nz, kb)), axis=0)
        part = after(part, two, *early)
        four = send(after(two, part), late_steps[2])
        last = [
            send(after(jnp.concatenate([part_[2][:2], part_[3][:2]]), part), PARTNER)
            for part_ in near
        ]
        whole = along_z(jnp.broadcast_to(part, (nz,) + part.shape)).reshape(count, kb)
        whole = after(whole, four, three, *last)
        sums = lax.all_gather(whole, "prow", axis=0, tiled=True, axis_index_groups=in_chip)
        rest = send(sums[nblk * rows :], PARTNER)
        far = tuple(zip(early, last))
        group = (pair, two, three, four)
        return update(order, late, info, sums, rest, factors, eig, near, group, far)

    return jax.shard_map(
        per_device, mesh=mesh, in_specs=placed, out_specs=P("pcol", "prow"), check_vma=False
    )
```

```python
import jax
import jax.numpy as jnp
import numpy as np
from jax import lax
from jax.experimental import pallas as pl
from jax.experimental.pallas import tpu as pltpu
from jax.sharding import PartitionSpec as P

F32 = jnp.float32
BF16 = jnp.bfloat16
NT = (((1,), (1,)), ((), ()))
NN = (((1,), (0,)), ((), ()))
X_NEAR, X_WRAP, Y_NEAR, Y_WRAP = 4, 12, 1, 3
ROUTES = (
    ((X_NEAR, X_WRAP, Y_NEAR, Y_WRAP), (Y_NEAR, Y_WRAP, X_NEAR, X_WRAP)),
    ((X_WRAP, X_NEAR, Y_WRAP, Y_NEAR), (Y_WRAP, Y_NEAR, X_WRAP, X_NEAR)),
)
PARTNER = (Y_WRAP, X_WRAP)


def split(x):
    high = x.astype(BF16)
    low = (x - high.astype(F32)).astype(BF16)
    return high, low


def product(left, right, dims):
    def dot(x, y):
        return lax.dot_general(x, y, dims, preferred_element_type=F32)

    return dot(left[0], right[0]) + (dot(left[1], right[0]) + dot(left[0], right[1]))


def exact(left, right, dims):
    return lax.dot_general(
        left, right, dims, precision=lax.Precision.HIGHEST, preferred_element_type=F32
    )


def pair_list(nblk):
    return [(b, c) for b in range(nblk) for c in range(b + 1, nblk)]


def block_row(block, rows, kb):
    return block * kb + (rows if block > 0 else 0)


def arrival_order(route):
    order = [0]
    for mask in route:
        order = order + [mask ^ at for at in order]
    return order


def inner_kernel(part, data, order_ref, info_ref, eig_ref, *refs):
    first = part == 0
    bufs, refs = refs[:4], refs[4:]
    if first:
        sum_ref, fac_ref, vecs, high, low = refs
    else:
        before_ref, keep_ref, give_ref, vecs, high, low, sum_ref = refs
    rows, cols = eig_ref.shape
    owners, nblk, share, _ = vecs.shape
    kb = owners * share
    start = 0 if first else cols - data

    for k, buf in enumerate(bufs):
        for i in range(buf.shape[0]):
            vecs[order_ref[part, k * buf.shape[0] + i]] = buf[i]

    eig_rows = slice(kb, kb + rows)
    high[eig_rows], low[eig_rows] = split(eig_ref[:, start : start + data])
    block = []
    for b in range(nblk):
        at = block_row(b, rows, kb)
        block.append(slice(at, at + kb))
        high[block[b]], low[block[b]] = split(vecs[:, b, :, :data].reshape(kb, data))
    if first:
        for b in range(nblk):
            fac_ref[b] = vecs[:, b, :, data:].reshape(kb, kb)

    def inner(left, right):
        return product((high[left], low[left]), (high[right], low[right]), NT)

    def add(at, term):
        here = slice(at, at + term.shape[0])
        sum_ref[here] = term if first else before_ref[here] + term

    below = nblk * rows
    add(0, inner(eig_rows, block[0]))

    @pl.when(info_ref[0] == 0)
    def _():
        left = slice(0, kb + rows)
        out = inner(left, block[1])
        add(below, out[:kb])
        add(rows, out[kb:])
        out = inner(left, slice(block[2].start, block[3].stop))
        for c in (2, 3):
            lane = slice((c - 2) * kb, (c - 1) * kb)
            add(below + (c - 1) * kb, out[:kb, lane])
            add(c * rows, out[kb:, lane])

    @pl.when(info_ref[0] == 1)
    def _():
        add(rows, inner(eig_rows, block[1]))
        out = inner(slice(kb, block[2].stop), slice(block[2].start, block[3].stop))
        add(2 * rows, out[:rows, :kb])
        add(3 * rows, out[:rows, kb:])
        add(below, out[rows : rows + kb, :kb])
        add(below + kb, out[rows : rows + kb, kb:])
        add(below + 2 * kb, out[rows + kb :, kb:])

    if not first:
        half = keep_ref.shape[0]
        core = info_ref[1]
        keep_ref[...] = sum_ref[pl.ds(pl.multiple_of(core * half, 8), half)]
        give_ref[...] = sum_ref[pl.ds(pl.multiple_of((1 - core) * half, 8), half)]


def inner_sums(part, data, order, info, eig, bufs, before=None):
    rows, _ = eig.shape
    _, nblk, share, width = bufs[0].shape
    owners = sum(buf.shape[0] for buf in bufs)
    kb = owners * share
    depth = rows + nblk * kb
    count = nblk * rows + len(pair_list(nblk)) // 2 * kb
    vmem = pl.BlockSpec(memory_space=pltpu.VMEM)
    smem = pl.BlockSpec(memory_space=pltpu.SMEM)
    sums = jax.ShapeDtypeStruct((count, kb), F32)
    scratch = [pltpu.VMEM((owners, nblk, share, width), F32)]
    scratch += [pltpu.VMEM((depth, data), BF16)] * 2
    if part == 0:
        outs = [sums, jax.ShapeDtypeStruct((nblk, kb, kb), F32)]
    else:
        outs = [jax.ShapeDtypeStruct((count // 2, kb), F32)] * 2
        scratch.append(pltpu.VMEM((count, kb), F32))
    return pl.pallas_call(
        lambda *refs: inner_kernel(part, data, *refs),
        out_shape=outs,
        in_specs=[smem, smem] + [vmem] * (5 + part),
        out_specs=[vmem] * len(outs),
        scratch_shapes=scratch,
        compiler_params=pltpu.CompilerParams(vmem_limit_bytes=24 * 2**20),
        cost_estimate=pl.CostEstimate(
            flops=6 * data * kb * count, bytes_accessed=4 * data * depth, transcendentals=0
        ),
        name="inner_sums",
    )(order, info, eig, *bufs, *([before] if part == 1 else []))


def owner_copies(order_ref, part, bufs, into, sems):
    copies = []
    for k, buf in enumerate(bufs):
        for i in range(buf.shape[0]):
            slot = k * buf.shape[0] + i
            copies.append(
                pltpu.make_async_copy(
                    buf.at[i], into.at[order_ref[part, slot]], sems.at[part, slot]
                )
            )
    return copies


def update_kernel(order_ref, info_ref, sum_ref, rest_ref, fac_ref, eig_ref, *refs):
    bufs = (refs[0:4], refs[4:8])
    out_ref, vecs, out, high, low, sems, out_sems = refs[8], refs[9:11], *refs[11:]
    rows, cols = eig_ref.shape
    nblk, kb, _ = fac_ref.shape
    below = nblk * rows
    pairs = pair_list(nblk)
    parity = info_ref[0]
    width_b = vecs[1].shape[3]
    spans = ((0, cols - width_b), (cols - width_b, width_b))

    copies = [owner_copies(order_ref, part, bufs[part], vecs[part], sems) for part in range(2)]
    for copy in copies[0] + copies[1]:
        copy.start()

    scaled = []
    for c in range(nblk):
        proj = sum_ref[c * rows : (c + 1) * rows]
        for b in range(c):
            index = pairs.index((b, c))
            at = index % (len(pairs) // 2) * kb
            mine = sum_ref[below + at : below + at + kb]
            rest = rest_ref[at : at + kb]
            gram = jnp.where((parity == 0) == (index < len(pairs) // 2), mine, rest)
            proj = proj - exact(scaled[b], gram, NN)
        scaled.append(exact(proj, fac_ref[c], NT))
        lane = slice(c * kb, (c + 1) * kb)
        high[:, lane], low[:, lane] = split(scaled[c])

    left = (high[...], low[...])
    out_copies = []
    for part, (start, width) in enumerate(spans):
        for copy in copies[part]:
            copy.wait()
        for at in range(0, width, 256):
            size = min(256, width - at)
            here = slice(start + at, start + at + size)
            right = jnp.concatenate(
                [vecs[part][:, b, :, at : at + size].reshape(kb, size) for b in range(nblk)],
                axis=0,
            )
            out[:, here] = eig_ref[:, here] - product(left, split(right), NN)
        lane = pl.ds(start, width)
        out_copies.append(
            pltpu.make_async_copy(out.at[:, lane], out_ref.at[:, lane], out_sems.at[part])
        )
        out_copies[part].start()
    for copy in out_copies:
        copy.wait()


def update(order, info, sums, rest, factors, eig, parts):
    rows, cols = eig.shape
    nblk, kb, _ = factors.shape
    _, _, share, _ = parts[0][0].shape
    owners = kb // share
    vmem = pl.BlockSpec(memory_space=pltpu.VMEM)
    smem = pl.BlockSpec(memory_space=pltpu.SMEM)
    hbm = pl.BlockSpec(memory_space=pl.ANY)
    return pl.pallas_call(
        update_kernel,
        out_shape=jax.ShapeDtypeStruct(eig.shape, F32),
        in_specs=[smem] * 2 + [vmem] * 4 + [hbm] * 8,
        out_specs=hbm,
        scratch_shapes=[
            pltpu.VMEM((owners, nblk, share, parts[0][0].shape[3]), F32),
            pltpu.VMEM((owners, nblk, share, parts[1][0].shape[3]), F32),
            pltpu.VMEM((rows, cols), F32),
            pltpu.VMEM((rows, nblk * kb), BF16),
            pltpu.VMEM((rows, nblk * kb), BF16),
            pltpu.SemaphoreType.DMA((2, owners)),
            pltpu.SemaphoreType.DMA((2,)),
        ],
        compiler_params=pltpu.CompilerParams(vmem_limit_bytes=40 * 2**20),
        cost_estimate=pl.CostEstimate(
            flops=6 * rows * nblk * kb * cols,
            bytes_accessed=4 * cols * (2 * rows + nblk * kb),
            transcendentals=0,
        ),
        name="update",
    )(order, info, sums, rest, factors, eig, *parts[0], *parts[1])


def solution(mesh):
    placed = (P("pcol", "prow"), P(None, "pcol", "prow"), P(None, "pcol", None))
    nprow, npcol = mesh.shape["prow"], mesh.shape["pcol"]
    nz = nprow // 2
    orders = np.array([[arrival_order(route) for route in routes] for routes in ROUTES], np.int32)
    in_chip = [[2 * z, 2 * z + 1] for z in range(nz)]

    def send(x, masks):
        pairs = []
        for row in range(nprow):
            mask = masks[row % 2]
            pairs += [(row * npcol + at, row * npcol + (at ^ mask)) for at in range(npcol)]
        return lax.ppermute(x, ("prow", "pcol"), pairs)

    def gather_in_plane(own, part):
        steps = [(ROUTES[part][0][n], ROUTES[part][1][n]) for n in range(4)]
        held = own[None]
        held = jnp.concatenate([held, send(held, steps[0])], axis=0)
        held = jnp.concatenate([held, send(held, steps[1])], axis=0)
        third = send(held, steps[2])
        return held, third, send(held, steps[3]), send(third, steps[3])

    def along_z(x):
        groups = [list(range(core, nprow, 2)) for core in range(2)]
        return lax.all_to_all(x, "prow", 0, 0, axis_index_groups=groups)

    def sum_over_rows(keep, give):
        half, kb = keep.shape
        mine = keep + lax.ppermute(give, "prow", [(i, i ^ 1) for i in range(nprow)])
        part = jnp.sum(along_z(mine.reshape(nz, half // nz, kb)), axis=0)
        whole = along_z(jnp.broadcast_to(part, (nz,) + part.shape)).reshape(half, kb)
        return lax.all_gather(whole, "prow", axis=0, tiled=True, axis_index_groups=in_chip)

    def per_device(eig, house_vecs, wy_factor):
        nblk, _, kb = wy_factor.shape
        rows, cols = eig.shape
        data = (cols // 128 - 1) // 2 * 128
        at = lax.axis_index("pcol").astype(jnp.int32)
        core = lax.rem(lax.axis_index("prow"), 2).astype(jnp.int32)
        parity = jnp.bitwise_and(jnp.bitwise_xor(at >> 1, at >> 3), 1)
        info = jnp.stack([parity, core])
        order = jnp.bitwise_xor(at, jnp.where(core == 0, orders[:, 0], orders[:, 1]))
        own_a = jnp.concatenate([house_vecs[:, :, :data], wy_factor], axis=2)
        own_b = house_vecs[:, :, data:]
        part_a = gather_in_plane(own_a, 0)
        part_b = gather_in_plane(own_b, 1)
        order_a, third_b = lax.optimization_barrier((order, part_b[2]))
        part_b = part_b[:2] + (third_b,) + part_b[3:]
        before, factors = inner_sums(0, data, order_a, info, eig, part_a)
        keep, give = inner_sums(1, cols - data, order, info, eig, part_b, before)
        sums = sum_over_rows(keep, give)
        rest = send(sums[nblk * rows :], PARTNER)
        return update(order, info, sums, rest, factors, eig, (part_a, part_b))

    return jax.shard_map(
        per_device, mesh=mesh, in_specs=placed, out_specs=P("pcol", "prow"), check_vma=False
    )
```

```python
import jax
import jax.numpy as jnp
import numpy as np
from jax import lax
from jax.experimental import pallas as pl
from jax.experimental.pallas import tpu as pltpu
from jax.sharding import PartitionSpec as P

F32 = jnp.float32
BF16 = jnp.bfloat16
NT = (((1,), (1,)), ((), ()))
NN = (((1,), (0,)), ((), ()))
X_NEAR, X_WRAP, Y_NEAR, Y_WRAP = 4, 12, 1, 3
ROUTES = (
    ((X_NEAR, X_WRAP, Y_NEAR, Y_WRAP), (Y_NEAR, Y_WRAP, X_NEAR, X_WRAP)),
    ((X_WRAP, X_NEAR, Y_WRAP, Y_NEAR), (Y_WRAP, Y_NEAR, X_WRAP, X_NEAR)),
)
PARTNER = (Y_WRAP, X_WRAP)


def split(x):
    high = x.astype(BF16)
    low = (x - high.astype(F32)).astype(BF16)
    return high, low


def product(left, right, dims):
    rows = left[0].shape[0]
    both = lax.dot_general(
        jnp.concatenate(left, axis=0), right[0], dims, preferred_element_type=F32
    )
    cross = lax.dot_general(left[0], right[1], dims, preferred_element_type=F32)
    return both[:rows] + (both[rows:] + cross)


def exact(left, right, dims):
    return lax.dot_general(
        left, right, dims, precision=lax.Precision.HIGHEST, preferred_element_type=F32
    )


def pair_list(nblk):
    return [(b, c) for b in range(nblk) for c in range(b + 1, nblk)]


def block_row(block, rows, kb):
    return block * kb + (rows if block > 0 else 0)


def arrival_order(route):
    order = [0]
    for mask in route:
        order = order + [mask ^ at for at in order]
    return order


def owner_copies(order_ref, part, bufs, into, sems):
    copies = []
    for k, buf in enumerate(bufs):
        for i in range(buf.shape[0]):
            slot = k * buf.shape[0] + i
            copies.append(
                pltpu.make_async_copy(
                    buf.at[i], into.at[order_ref[part, slot]], sems.at[part, slot]
                )
            )
    return copies


def collect_kernel(part, order_ref, *refs):
    bufs, out_ref, sems = refs[:-2], refs[-2], refs[-1]
    copies = owner_copies(order_ref, part, bufs, out_ref, sems)
    for copy in copies:
        copy.start()
    for copy in copies:
        copy.wait()


def collect(part, order, bufs):
    _, nblk, share, width = bufs[0].shape
    owners = order.shape[1]
    return pl.pallas_call(
        lambda *refs: collect_kernel(part, *refs),
        out_shape=jax.ShapeDtypeStruct((owners, nblk, share, width), F32),
        in_specs=[pl.BlockSpec(memory_space=pltpu.SMEM)]
        + [pl.BlockSpec(memory_space=pl.ANY)] * len(bufs),
        out_specs=pl.BlockSpec(memory_space=pltpu.VMEM),
        scratch_shapes=[pltpu.SemaphoreType.DMA((2, owners))],
        compiler_params=pltpu.CompilerParams(vmem_limit_bytes=8 * 2**20),
        cost_estimate=pl.CostEstimate(
            flops=0, bytes_accessed=8 * owners * nblk * share * width, transcendentals=0
        ),
        name="collect",
    )(order, *bufs)


def inner_kernel(part, data, order_ref, info_ref, eig_ref, *refs):
    first = part == 0
    early_ref, late_ref, refs = refs[0], refs[1], refs[2:]
    if first:
        sum_ref, fac_ref, vecs, high, low = refs
    else:
        before_ref, keep_ref, give_ref, vecs, high, low, sum_ref = refs
    rows, cols = eig_ref.shape
    owners, nblk, share, _ = vecs.shape
    kb = owners * share
    start = 0 if first else cols - data

    vecs[...] = early_ref[...]
    count = late_ref.shape[0]
    for i in range(count):
        vecs[order_ref[part, owners - count + i]] = late_ref[i]

    eig_rows = slice(kb, kb + rows)
    high[eig_rows], low[eig_rows] = split(eig_ref[:, start : start + data])
    block = []
    for b in range(nblk):
        at = block_row(b, rows, kb)
        block.append(slice(at, at + kb))
        for owner in range(0, owners, 2):
            two = vecs[owner : owner + 2, b, :, :data].reshape(2 * share, data)
            here = slice(at + owner * share, at + (owner + 2) * share)
            high[here], low[here] = split(two)
    if first:
        for b in range(nblk):
            fac_ref[b] = vecs[:, b, :, data:].reshape(kb, kb)

    def inner(left, right):
        return product((high[left], low[left]), (high[right], low[right]), NT)

    def add(at, term):
        here = slice(at, at + term.shape[0])
        sum_ref[here] = term if first else before_ref[here] + term

    below = nblk * rows
    add(0, inner(eig_rows, block[0]))

    @pl.when(info_ref[0] == 0)
    def _():
        left = slice(0, kb + rows)
        out = inner(left, block[1])
        add(below, out[:kb])
        add(rows, out[kb:])
        out = inner(left, slice(block[2].start, block[3].stop))
        for c in (2, 3):
            lane = slice((c - 2) * kb, (c - 1) * kb)
            add(below + (c - 1) * kb, out[:kb, lane])
            add(c * rows, out[kb:, lane])

    @pl.when(info_ref[0] == 1)
    def _():
        add(rows, inner(eig_rows, block[1]))
        out = inner(slice(kb, block[2].stop), slice(block[2].start, block[3].stop))
        add(2 * rows, out[:rows, :kb])
        add(3 * rows, out[:rows, kb:])
        add(below, out[rows : rows + kb, :kb])
        add(below + kb, out[rows : rows + kb, kb:])
        add(below + 2 * kb, out[rows + kb :, kb:])

    if not first:
        half = keep_ref.shape[0]
        core = info_ref[1]
        keep_ref[...] = sum_ref[pl.ds(pl.multiple_of(core * half, 8), half)]
        give_ref[...] = sum_ref[pl.ds(pl.multiple_of((1 - core) * half, 8), half)]


def inner_sums(part, data, order, info, eig, bufs, before=None):
    rows, _ = eig.shape
    _, nblk, share, width = bufs[-1].shape
    owners = order.shape[1]
    kb = owners * share
    depth = rows + nblk * kb
    count = nblk * rows + len(pair_list(nblk)) // 2 * kb
    vmem = pl.BlockSpec(memory_space=pltpu.VMEM)
    smem = pl.BlockSpec(memory_space=pltpu.SMEM)
    sums = jax.ShapeDtypeStruct((count, kb), F32)
    scratch = [pltpu.VMEM((owners, nblk, share, width), F32)]
    scratch += [pltpu.VMEM((depth, data), BF16)] * 2
    if part == 0:
        outs = [sums, jax.ShapeDtypeStruct((nblk, kb, kb), F32)]
    else:
        outs = [jax.ShapeDtypeStruct((count // 2, kb), F32)] * 2
        scratch.append(pltpu.VMEM((count, kb), F32))
    return pl.pallas_call(
        lambda *refs: inner_kernel(part, data, *refs),
        out_shape=outs,
        in_specs=[smem, smem] + [vmem] * (1 + len(bufs) + part),
        out_specs=[vmem] * len(outs),
        scratch_shapes=scratch,
        compiler_params=pltpu.CompilerParams(vmem_limit_bytes=24 * 2**20),
        cost_estimate=pl.CostEstimate(
            flops=6 * data * kb * count, bytes_accessed=4 * data * depth, transcendentals=0
        ),
        name="inner_sums",
    )(order, info, eig, *bufs, *([before] if part == 1 else []))


def update_kernel(order_ref, info_ref, sum_ref, rest_ref, fac_ref, eig_ref, *refs):
    bufs = (refs[0:4], refs[4:8])
    out_ref, vecs, out, high, low, sems, out_sems = refs[8], refs[9:11], *refs[11:]
    rows, cols = eig_ref.shape
    nblk, kb, _ = fac_ref.shape
    below = nblk * rows
    pairs = pair_list(nblk)
    parity = info_ref[0]
    width_b = vecs[1].shape[3]
    spans = ((0, cols - width_b), (cols - width_b, width_b))

    copies = [owner_copies(order_ref, part, bufs[part], vecs[part], sems) for part in range(2)]
    for copy in copies[0] + copies[1]:
        copy.start()

    scaled = []
    for c in range(nblk):
        proj = sum_ref[c * rows : (c + 1) * rows]
        for b in range(c):
            index = pairs.index((b, c))
            at = index % (len(pairs) // 2) * kb
            mine = sum_ref[below + at : below + at + kb]
            rest = rest_ref[at : at + kb]
            gram = jnp.where((parity == 0) == (index < len(pairs) // 2), mine, rest)
            proj = proj - exact(scaled[b], gram, NN)
        scaled.append(exact(proj, fac_ref[c], NT))
        lane = slice(c * kb, (c + 1) * kb)
        high[:, lane], low[:, lane] = split(scaled[c])

    left = (high[...], low[...])
    out_copies = []
    for part, (start, width) in enumerate(spans):
        for copy in copies[part]:
            copy.wait()
        for at in range(0, width, 256):
            size = min(256, width - at)
            here = slice(start + at, start + at + size)
            right = jnp.concatenate(
                [vecs[part][:, b, :, at : at + size].reshape(kb, size) for b in range(nblk)],
                axis=0,
            )
            out[:, here] = eig_ref[:, here] - product(left, split(right), NN)
        lane = pl.ds(start, width)
        out_copies.append(
            pltpu.make_async_copy(out.at[:, lane], out_ref.at[:, lane], out_sems.at[part])
        )
        out_copies[part].start()
    for copy in out_copies:
        copy.wait()


def update(order, info, sums, rest, factors, eig, parts):
    rows, cols = eig.shape
    nblk, kb, _ = factors.shape
    _, _, share, _ = parts[0][0].shape
    owners = kb // share
    vmem = pl.BlockSpec(memory_space=pltpu.VMEM)
    smem = pl.BlockSpec(memory_space=pltpu.SMEM)
    hbm = pl.BlockSpec(memory_space=pl.ANY)
    return pl.pallas_call(
        update_kernel,
        out_shape=jax.ShapeDtypeStruct(eig.shape, F32),
        in_specs=[smem] * 2 + [vmem] * 4 + [hbm] * 8,
        out_specs=hbm,
        scratch_shapes=[
            pltpu.VMEM((owners, nblk, share, parts[0][0].shape[3]), F32),
            pltpu.VMEM((owners, nblk, share, parts[1][0].shape[3]), F32),
            pltpu.VMEM((rows, cols), F32),
            pltpu.VMEM((rows, nblk * kb), BF16),
            pltpu.VMEM((rows, nblk * kb), BF16),
            pltpu.SemaphoreType.DMA((2, owners)),
            pltpu.SemaphoreType.DMA((2,)),
        ],
        compiler_params=pltpu.CompilerParams(vmem_limit_bytes=40 * 2**20),
        cost_estimate=pl.CostEstimate(
            flops=6 * rows * nblk * kb * cols,
            bytes_accessed=4 * cols * (2 * rows + nblk * kb),
            transcendentals=0,
        ),
        name="update",
    )(order, info, sums, rest, factors, eig, *parts[0], *parts[1])


def solution(mesh):
    placed = (P("pcol", "prow"), P(None, "pcol", "prow"), P(None, "pcol", None))
    nprow, npcol = mesh.shape["prow"], mesh.shape["pcol"]
    nz = nprow // 2
    orders = np.array([[arrival_order(route) for route in routes] for routes in ROUTES], np.int32)
    in_chip = [[2 * z, 2 * z + 1] for z in range(nz)]

    def send(x, masks):
        pairs = []
        for row in range(nprow):
            mask = masks[row % 2]
            pairs += [(row * npcol + at, row * npcol + (at ^ mask)) for at in range(npcol)]
        return lax.ppermute(x, ("prow", "pcol"), pairs)

    def gather_in_plane(own, part):
        steps = [(ROUTES[part][0][n], ROUTES[part][1][n]) for n in range(4)]
        held = own[None]
        held = jnp.concatenate([held, send(held, steps[0])], axis=0)
        held = jnp.concatenate([held, send(held, steps[1])], axis=0)
        third = send(held, steps[2])
        return held, third, send(held, steps[3]), send(third, steps[3])

    def along_z(x):
        groups = [list(range(core, nprow, 2)) for core in range(2)]
        return lax.all_to_all(x, "prow", 0, 0, axis_index_groups=groups)

    def sum_over_rows(keep, give):
        half, kb = keep.shape
        mine = keep + lax.ppermute(give, "prow", [(i, i ^ 1) for i in range(nprow)])
        part = jnp.sum(along_z(mine.reshape(nz, half // nz, kb)), axis=0)
        whole = along_z(jnp.broadcast_to(part, (nz,) + part.shape)).reshape(half, kb)
        return lax.all_gather(whole, "prow", axis=0, tiled=True, axis_index_groups=in_chip)

    def per_device(eig, house_vecs, wy_factor):
        nblk, _, kb = wy_factor.shape
        rows, cols = eig.shape
        data = (cols // 128 - 1) // 2 * 128
        at = lax.axis_index("pcol").astype(jnp.int32)
        core = lax.rem(lax.axis_index("prow"), 2).astype(jnp.int32)
        parity = jnp.bitwise_and(jnp.bitwise_xor(at >> 1, at >> 3), 1)
        info = jnp.stack([parity, core])
        order = jnp.bitwise_xor(at, jnp.where(core == 0, orders[:, 0], orders[:, 1]))
        own_a = jnp.concatenate([house_vecs[:, :, :data], wy_factor], axis=2)
        own_b = house_vecs[:, :, data:]
        part_a = gather_in_plane(own_a, 0)
        part_b = gather_in_plane(own_b, 1)
        early_a = collect(0, order, part_a[:3])
        early_b = collect(1, order, part_b[:3])
        order_a, early_b = lax.optimization_barrier((order, early_b))
        before, factors = inner_sums(0, data, order_a, info, eig, (early_a, part_a[3]))
        keep, give = inner_sums(
            1, cols - data, order, info, eig, (early_b, part_b[3]), before
        )
        sums = sum_over_rows(keep, give)
        rest = send(sums[nblk * rows :], PARTNER)
        return update(order, info, sums, rest, factors, eig, (part_a, part_b))

    return jax.shard_map(
        per_device, mesh=mesh, in_specs=placed, out_specs=P("pcol", "prow"), check_vma=False
    )
```

```python
import jax
import jax.numpy as jnp
import numpy as np
from jax import lax
from jax.experimental import pallas as pl
from jax.experimental.pallas import tpu as pltpu
from jax.sharding import PartitionSpec as P

F32 = jnp.float32
BF16 = jnp.bfloat16
NT = (((1,), (1,)), ((), ()))
NN = (((1,), (0,)), ((), ()))
X_NEAR, X_WRAP, Y_NEAR, Y_WRAP = 4, 12, 1, 3
ROUTES = (
    ((X_NEAR, X_WRAP, Y_NEAR, Y_WRAP), (Y_NEAR, Y_WRAP, X_NEAR, X_WRAP)),
    ((X_WRAP, X_NEAR, Y_WRAP, Y_NEAR), (Y_WRAP, Y_NEAR, X_WRAP, X_NEAR)),
)
PARTNER = X_WRAP


def split(x):
    high = x.astype(BF16)
    low = (x - high.astype(F32)).astype(BF16)
    return high, low


def product(left, right, dims):
    rows = left[0].shape[0]
    both = lax.dot_general(
        jnp.concatenate(left, axis=0), right[0], dims, preferred_element_type=F32
    )
    cross = lax.dot_general(left[0], right[1], dims, preferred_element_type=F32)
    return both[:rows] + (both[rows:] + cross)


def exact(left, right, dims):
    return lax.dot_general(
        left, right, dims, precision=lax.Precision.HIGHEST, preferred_element_type=F32
    )


def pair_list(nblk):
    return [(b, c) for b in range(nblk) for c in range(b + 1, nblk)]


def block_row(block, rows, kb):
    return block * kb + (rows if block > 0 else 0)


def arrival_order(route):
    order = [0]
    for mask in route:
        order = order + [mask ^ at for at in order]
    return order


def owner_copies(order_ref, part, bufs, into, sems):
    copies = []
    for k, buf in enumerate(bufs):
        for i in range(buf.shape[0]):
            slot = k * buf.shape[0] + i
            copies.append(
                pltpu.make_async_copy(
                    buf.at[i], into.at[order_ref[part, slot]], sems.at[part, slot]
                )
            )
    return copies


def collect_kernel(part, order_ref, *refs):
    bufs, out_ref, sems = refs[:-2], refs[-2], refs[-1]
    copies = owner_copies(order_ref, part, bufs, out_ref, sems)
    for copy in copies:
        copy.start()
    for copy in copies:
        copy.wait()


def collect(part, order, bufs):
    _, nblk, share, width = bufs[0].shape
    owners = order.shape[1]
    return pl.pallas_call(
        lambda *refs: collect_kernel(part, *refs),
        out_shape=jax.ShapeDtypeStruct((owners, nblk, share, width), F32),
        in_specs=[pl.BlockSpec(memory_space=pltpu.SMEM)]
        + [pl.BlockSpec(memory_space=pl.ANY)] * len(bufs),
        out_specs=pl.BlockSpec(memory_space=pltpu.VMEM),
        scratch_shapes=[pltpu.SemaphoreType.DMA((2, owners))],
        compiler_params=pltpu.CompilerParams(vmem_limit_bytes=8 * 2**20),
        cost_estimate=pl.CostEstimate(
            flops=0, bytes_accessed=8 * owners * nblk * share * width, transcendentals=0
        ),
        name="collect",
    )(order, *bufs)


def inner_kernel(part, data, order_ref, info_ref, eig_ref, *refs):
    first = part == 0
    early_ref, late_ref, refs = refs[0], refs[1], refs[2:]
    if first:
        sum_ref, fac_ref, vecs, high, low = refs
    else:
        before_ref, keep_ref, give_ref, vecs, high, low, sum_ref = refs
    rows, cols = eig_ref.shape
    owners, nblk, share, _ = vecs.shape
    kb = owners * share
    start = 0 if first else cols - data

    vecs[...] = early_ref[...]
    count = late_ref.shape[0]
    for i in range(count):
        vecs[order_ref[part, owners - count + i]] = late_ref[i]

    eig_rows = slice(kb, kb + rows)
    high[eig_rows], low[eig_rows] = split(eig_ref[:, start : start + data])
    block = []
    for b in range(nblk):
        at = block_row(b, rows, kb)
        block.append(slice(at, at + kb))
        for owner in range(0, owners, 2):
            two = vecs[owner : owner + 2, b, :, :data].reshape(2 * share, data)
            here = slice(at + owner * share, at + (owner + 2) * share)
            high[here], low[here] = split(two)
    if first:
        for b in range(nblk):
            fac_ref[b] = vecs[:, b, :, data:].reshape(kb, kb)

    def inner(left, right):
        return product((high[left], low[left]), (high[right], low[right]), NT)

    def add(at, term):
        here = slice(at, at + term.shape[0])
        sum_ref[here] = term if first else before_ref[here] + term

    below = nblk * rows
    add(0, inner(eig_rows, block[0]))

    @pl.when(info_ref[0] == 0)
    def _():
        left = slice(0, kb + rows)
        out = inner(left, block[1])
        add(below, out[:kb])
        add(rows, out[kb:])
        out = inner(left, slice(block[2].start, block[3].stop))
        for c in (2, 3):
            lane = slice((c - 2) * kb, (c - 1) * kb)
            add(below + (c - 1) * kb, out[:kb, lane])
            add(c * rows, out[kb:, lane])

    @pl.when(info_ref[0] == 1)
    def _():
        add(rows, inner(eig_rows, block[1]))
        out = inner(slice(kb, block[2].stop), slice(block[2].start, block[3].stop))
        add(2 * rows, out[:rows, :kb])
        add(3 * rows, out[:rows, kb:])
        add(below, out[rows : rows + kb, :kb])
        add(below + kb, out[rows : rows + kb, kb:])
        add(below + 2 * kb, out[rows + kb :, kb:])

    if not first:
        half = keep_ref.shape[0]
        core = info_ref[1]
        keep_ref[...] = sum_ref[pl.ds(pl.multiple_of(core * half, 8), half)]
        give_ref[...] = sum_ref[pl.ds(pl.multiple_of((1 - core) * half, 8), half)]


def inner_sums(part, data, order, info, eig, bufs, before=None):
    rows, _ = eig.shape
    _, nblk, share, width = bufs[-1].shape
    owners = order.shape[1]
    kb = owners * share
    depth = rows + nblk * kb
    count = nblk * rows + len(pair_list(nblk)) // 2 * kb
    vmem = pl.BlockSpec(memory_space=pltpu.VMEM)
    smem = pl.BlockSpec(memory_space=pltpu.SMEM)
    sums = jax.ShapeDtypeStruct((count, kb), F32)
    scratch = [pltpu.VMEM((owners, nblk, share, width), F32)]
    scratch += [pltpu.VMEM((depth, data), BF16)] * 2
    if part == 0:
        outs = [sums, jax.ShapeDtypeStruct((nblk, kb, kb), F32)]
    else:
        outs = [jax.ShapeDtypeStruct((count // 2, kb), F32)] * 2
        scratch.append(pltpu.VMEM((count, kb), F32))
    return pl.pallas_call(
        lambda *refs: inner_kernel(part, data, *refs),
        out_shape=outs,
        in_specs=[smem, smem] + [vmem] * (1 + len(bufs) + part),
        out_specs=[vmem] * len(outs),
        scratch_shapes=scratch,
        compiler_params=pltpu.CompilerParams(vmem_limit_bytes=24 * 2**20),
        cost_estimate=pl.CostEstimate(
            flops=6 * data * kb * count, bytes_accessed=4 * data * depth, transcendentals=0
        ),
        name="inner_sums",
    )(order, info, eig, *bufs, *([before] if part == 1 else []))


def update_kernel(order_ref, info_ref, sum_ref, rest_ref, fac_ref, eig_ref, *refs):
    bufs = (refs[0:4], refs[4:8])
    out_ref, vecs, out, high, low, sems, out_sems = refs[8], refs[9:11], *refs[11:]
    rows, cols = eig_ref.shape
    nblk, kb, _ = fac_ref.shape
    below = nblk * rows
    pairs = pair_list(nblk)
    parity = info_ref[0]
    width_b = vecs[1].shape[3]
    spans = ((0, cols - width_b), (cols - width_b, width_b))

    copies = [owner_copies(order_ref, part, bufs[part], vecs[part], sems) for part in range(2)]
    for copy in copies[0] + copies[1]:
        copy.start()

    scaled = []
    for c in range(nblk):
        proj = sum_ref[c * rows : (c + 1) * rows]
        for b in range(c):
            index = pairs.index((b, c))
            at = index % (len(pairs) // 2) * kb
            mine = sum_ref[below + at : below + at + kb]
            rest = rest_ref[at : at + kb]
            gram = jnp.where((parity == 0) == (index < len(pairs) // 2), mine, rest)
            proj = proj - exact(scaled[b], gram, NN)
        scaled.append(exact(proj, fac_ref[c], NT))
        lane = slice(c * kb, (c + 1) * kb)
        high[:, lane], low[:, lane] = split(scaled[c])

    left = (high[...], low[...])
    out_copies = []
    for part, (start, width) in enumerate(spans):
        for copy in copies[part]:
            copy.wait()
        for at in range(0, width, 256):
            size = min(256, width - at)
            here = slice(start + at, start + at + size)
            right = jnp.concatenate(
                [vecs[part][:, b, :, at : at + size].reshape(kb, size) for b in range(nblk)],
                axis=0,
            )
            out[:, here] = eig_ref[:, here] - product(left, split(right), NN)
        lane = pl.ds(start, width)
        out_copies.append(
            pltpu.make_async_copy(out.at[:, lane], out_ref.at[:, lane], out_sems.at[part])
        )
        out_copies[part].start()
    for copy in out_copies:
        copy.wait()


def update(order, info, sums, rest, factors, eig, parts):
    rows, cols = eig.shape
    nblk, kb, _ = factors.shape
    _, _, share, _ = parts[0][0].shape
    owners = kb // share
    vmem = pl.BlockSpec(memory_space=pltpu.VMEM)
    smem = pl.BlockSpec(memory_space=pltpu.SMEM)
    hbm = pl.BlockSpec(memory_space=pl.ANY)
    return pl.pallas_call(
        update_kernel,
        out_shape=jax.ShapeDtypeStruct(eig.shape, F32),
        in_specs=[smem] * 2 + [vmem] * 4 + [hbm] * 8,
        out_specs=hbm,
        scratch_shapes=[
            pltpu.VMEM((owners, nblk, share, parts[0][0].shape[3]), F32),
            pltpu.VMEM((owners, nblk, share, parts[1][0].shape[3]), F32),
            pltpu.VMEM((rows, cols), F32),
            pltpu.VMEM((rows, nblk * kb), BF16),
            pltpu.VMEM((rows, nblk * kb), BF16),
            pltpu.SemaphoreType.DMA((2, owners)),
            pltpu.SemaphoreType.DMA((2,)),
        ],
        compiler_params=pltpu.CompilerParams(vmem_limit_bytes=40 * 2**20),
        cost_estimate=pl.CostEstimate(
            flops=6 * rows * nblk * kb * cols,
            bytes_accessed=4 * cols * (2 * rows + nblk * kb),
            transcendentals=0,
        ),
        name="update",
    )(order, info, sums, rest, factors, eig, *parts[0], *parts[1])


def solution(mesh):
    placed = (P("pcol", "prow"), P(None, "pcol", "prow"), P(None, "pcol", None))
    nprow, npcol = mesh.shape["prow"], mesh.shape["pcol"]
    nz = nprow // 2
    orders = np.array([[arrival_order(route) for route in routes] for routes in ROUTES], np.int32)
    in_chip = [[2 * z, 2 * z + 1] for z in range(nz)]

    def send(x, masks):
        pairs = []
        for row in range(nprow):
            mask = masks[row % 2]
            pairs += [(row * npcol + at, row * npcol + (at ^ mask)) for at in range(npcol)]
        return lax.ppermute(x, ("prow", "pcol"), pairs)

    def gather_in_plane(own, part):
        steps = [(ROUTES[part][0][n], ROUTES[part][1][n]) for n in range(4)]
        held = own[None]
        held = jnp.concatenate([held, send(held, steps[0])], axis=0)
        held = jnp.concatenate([held, send(held, steps[1])], axis=0)
        third = send(held, steps[2])
        return held, third, send(held, steps[3]), send(third, steps[3])

    def along_z(x):
        groups = [list(range(core, nprow, 2)) for core in range(2)]
        return lax.all_to_all(x, "prow", 0, 0, axis_index_groups=groups)

    def sum_over_rows(keep, give):
        half, kb = keep.shape
        mine = keep + lax.ppermute(give, "prow", [(i, i ^ 1) for i in range(nprow)])
        part = jnp.sum(along_z(mine.reshape(nz, half // nz, kb)), axis=0)
        whole = along_z(jnp.broadcast_to(part, (nz,) + part.shape)).reshape(half, kb)
        pairs = [
            (row * npcol + at, row * npcol + (at ^ PARTNER))
            for row in range(1, nprow, 2)
            for at in range(npcol)
        ]
        other = lax.ppermute(whole, ("prow", "pcol"), pairs)
        sums = lax.all_gather(whole, "prow", axis=0, tiled=True, axis_index_groups=in_chip)
        sums, other = lax.optimization_barrier((sums, other))
        rest = lax.all_gather(other, "prow", axis=0, tiled=True, axis_index_groups=in_chip)
        return sums, rest[half:]

    def per_device(eig, house_vecs, wy_factor):
        nblk, _, kb = wy_factor.shape
        rows, cols = eig.shape
        data = (cols // 128 - 1) // 2 * 128
        at = lax.axis_index("pcol").astype(jnp.int32)
        core = lax.rem(lax.axis_index("prow"), 2).astype(jnp.int32)
        parity = jnp.bitwise_and(jnp.bitwise_xor(at >> 1, at >> 3), 1)
        info = jnp.stack([parity, core])
        order = jnp.bitwise_xor(at, jnp.where(core == 0, orders[:, 0], orders[:, 1]))
        own_a = jnp.concatenate([house_vecs[:, :, :data], wy_factor], axis=2)
        own_b = house_vecs[:, :, data:]
        part_a = gather_in_plane(own_a, 0)
        part_b = gather_in_plane(own_b, 1)
        early_a = collect(0, order, part_a[:3])
        early_b = collect(1, order, part_b[:3])
        order_a, early_b = lax.optimization_barrier((order, early_b))
        before, factors = inner_sums(0, data, order_a, info, eig, (early_a, part_a[3]))
        keep, give = inner_sums(
            1, cols - data, order, info, eig, (early_b, part_b[3]), before
        )
        sums, rest = sum_over_rows(keep, give)
        return update(order, info, sums, rest, factors, eig, (part_a, part_b))

    return jax.shard_map(
        per_device, mesh=mesh, in_specs=placed, out_specs=P("pcol", "prow"), check_vma=False
    )
```

```python
import jax
import jax.numpy as jnp
import numpy as np
from jax import lax
from jax.experimental import pallas as pl
from jax.experimental.pallas import tpu as pltpu
from jax.sharding import PartitionSpec as P

F32 = jnp.float32
BF16 = jnp.bfloat16
NT = (((1,), (1,)), ((), ()))
NN = (((1,), (0,)), ((), ()))
X_NEAR, X_WRAP, Y_NEAR, Y_WRAP = 4, 12, 1, 3
ROUTES = (
    ((X_NEAR, X_WRAP, Y_NEAR, Y_WRAP), (Y_NEAR, Y_WRAP, X_NEAR, X_WRAP)),
    ((X_WRAP, X_NEAR, Y_WRAP, Y_NEAR), (Y_WRAP, Y_NEAR, X_WRAP, X_NEAR)),
)
PARTNER = X_WRAP


def split(x):
    high = x.astype(BF16)
    low = (x - high.astype(F32)).astype(BF16)
    return high, low


def product(left, right, dims):
    rows = left[0].shape[0]
    both = lax.dot_general(
        jnp.concatenate(left, axis=0), right[0], dims, preferred_element_type=F32
    )
    cross = lax.dot_general(left[0], right[1], dims, preferred_element_type=F32)
    return both[:rows] + (both[rows:] + cross)


def exact(left, right, dims):
    return lax.dot_general(
        left, right, dims, precision=lax.Precision.HIGHEST, preferred_element_type=F32
    )


def pair_list(nblk):
    return [(b, c) for b in range(nblk) for c in range(b + 1, nblk)]


def block_row(block, rows, kb):
    return block * kb + (rows if block > 0 else 0)


def arrival_order(route):
    order = [0]
    for mask in route:
        order = order + [mask ^ at for at in order]
    return order


def owner_copies(order_ref, part, bufs, into, sems):
    copies = []
    for k, buf in enumerate(bufs):
        for i in range(buf.shape[0]):
            slot = k * buf.shape[0] + i
            copies.append(
                pltpu.make_async_copy(
                    buf.at[i], into.at[order_ref[part, slot]], sems.at[part, slot]
                )
            )
    return copies


def collect_kernel(part, order_ref, *refs):
    bufs, out_ref, sems = refs[:-2], refs[-2], refs[-1]
    copies = owner_copies(order_ref, part, bufs, out_ref, sems)
    for copy in copies:
        copy.start()
    for copy in copies:
        copy.wait()


def collect(part, order, bufs):
    _, nblk, share, width = bufs[0].shape
    owners = order.shape[1]
    return pl.pallas_call(
        lambda *refs: collect_kernel(part, *refs),
        out_shape=jax.ShapeDtypeStruct((owners, nblk, share, width), F32),
        in_specs=[pl.BlockSpec(memory_space=pltpu.SMEM)]
        + [pl.BlockSpec(memory_space=pl.ANY)] * len(bufs),
        out_specs=pl.BlockSpec(memory_space=pltpu.VMEM),
        scratch_shapes=[pltpu.SemaphoreType.DMA((2, owners))],
        compiler_params=pltpu.CompilerParams(vmem_limit_bytes=8 * 2**20),
        cost_estimate=pl.CostEstimate(
            flops=0, bytes_accessed=8 * owners * nblk * share * width, transcendentals=0
        ),
        name="collect",
    )(order, *bufs)


def inner_kernel(part, data, order_ref, info_ref, eig_ref, *refs):
    first = part == 0
    early_ref, late_ref, refs = refs[0], refs[1], refs[2:]
    if first:
        sum_ref, fac_ref, vecs, high, low = refs
    else:
        before_ref, keep_ref, give_ref, vecs, high, low, sum_ref = refs
    rows, cols = eig_ref.shape
    owners, nblk, share, _ = vecs.shape
    kb = owners * share
    start = 0 if first else cols - data

    vecs[...] = early_ref[...]
    count = late_ref.shape[0]
    for i in range(count):
        vecs[order_ref[part, owners - count + i]] = late_ref[i]

    eig_rows = slice(kb, kb + rows)
    high[eig_rows], low[eig_rows] = split(eig_ref[:, start : start + data])
    block = []
    for b in range(nblk):
        at = block_row(b, rows, kb)
        block.append(slice(at, at + kb))
        for owner in range(0, owners, 2):
            two = vecs[owner : owner + 2, b, :, :data].reshape(2 * share, data)
            here = slice(at + owner * share, at + (owner + 2) * share)
            high[here], low[here] = split(two)
    if first:
        for b in range(nblk):
            fac_ref[b] = vecs[:, b, :, data:].reshape(kb, kb)

    def inner(left, right):
        return product((high[left], low[left]), (high[right], low[right]), NT)

    def add(at, term):
        here = slice(at, at + term.shape[0])
        sum_ref[here] = term if first else before_ref[here] + term

    below = nblk * rows
    add(0, inner(eig_rows, block[0]))

    @pl.when(info_ref[0] == 0)
    def _():
        left = slice(0, kb + rows)
        out = inner(left, block[1])
        add(below, out[:kb])
        add(rows, out[kb:])
        out = inner(left, slice(block[2].start, block[3].stop))
        for c in (2, 3):
            lane = slice((c - 2) * kb, (c - 1) * kb)
            add(below + (c - 1) * kb, out[:kb, lane])
            add(c * rows, out[kb:, lane])

    @pl.when(info_ref[0] == 1)
    def _():
        add(rows, inner(eig_rows, block[1]))
        out = inner(slice(kb, block[2].stop), slice(block[2].start, block[3].stop))
        add(2 * rows, out[:rows, :kb])
        add(3 * rows, out[:rows, kb:])
        add(below, out[rows : rows + kb, :kb])
        add(below + kb, out[rows : rows + kb, kb:])
        add(below + 2 * kb, out[rows + kb :, kb:])

    if not first:
        half = keep_ref.shape[0]
        core = info_ref[1]
        keep_ref[...] = sum_ref[pl.ds(pl.multiple_of(core * half, 8), half)]
        give_ref[...] = sum_ref[pl.ds(pl.multiple_of((1 - core) * half, 8), half)]


def inner_sums(part, data, order, info, eig, bufs, before=None):
    rows, _ = eig.shape
    _, nblk, share, width = bufs[-1].shape
    owners = order.shape[1]
    kb = owners * share
    depth = rows + nblk * kb
    count = nblk * rows + len(pair_list(nblk)) // 2 * kb
    vmem = pl.BlockSpec(memory_space=pltpu.VMEM)
    smem = pl.BlockSpec(memory_space=pltpu.SMEM)
    sums = jax.ShapeDtypeStruct((count, kb), F32)
    scratch = [pltpu.VMEM((owners, nblk, share, width), F32)]
    scratch += [pltpu.VMEM((depth, data), BF16)] * 2
    if part == 0:
        outs = [sums, jax.ShapeDtypeStruct((nblk, kb, kb), F32)]
    else:
        outs = [jax.ShapeDtypeStruct((count // 2, kb), F32)] * 2
        scratch.append(pltpu.VMEM((count, kb), F32))
    return pl.pallas_call(
        lambda *refs: inner_kernel(part, data, *refs),
        out_shape=outs,
        in_specs=[smem, smem] + [vmem] * (1 + len(bufs) + part),
        out_specs=[vmem] * len(outs),
        scratch_shapes=scratch,
        compiler_params=pltpu.CompilerParams(vmem_limit_bytes=24 * 2**20),
        cost_estimate=pl.CostEstimate(
            flops=6 * data * kb * count, bytes_accessed=4 * data * depth, transcendentals=0
        ),
        name="inner_sums",
    )(order, info, eig, *bufs, *([before] if part == 1 else []))


def update_kernel(order_ref, info_ref, sum_ref, rest_ref, fac_ref, eig_ref, *refs):
    bufs = (refs[0:4], refs[4:8])
    out_ref, vecs, out, high, low, sems, out_sems = refs[8], refs[9:11], *refs[11:]
    rows, cols = eig_ref.shape
    nblk, kb, _ = fac_ref.shape
    below = nblk * rows
    pairs = pair_list(nblk)
    parity = info_ref[0]
    width_b = vecs[1].shape[3]
    spans = ((0, cols - width_b), (cols - width_b, width_b))

    copies = [owner_copies(order_ref, part, bufs[part], vecs[part], sems) for part in range(2)]
    for copy in copies[0] + copies[1]:
        copy.start()

    scaled = []
    for c in range(nblk):
        proj = sum_ref[c * rows : (c + 1) * rows]
        for b in range(c):
            index = pairs.index((b, c))
            at = index % (len(pairs) // 2) * kb
            mine = sum_ref[below + at : below + at + kb]
            rest = rest_ref[at : at + kb]
            gram = jnp.where((parity == 0) == (index < len(pairs) // 2), mine, rest)
            proj = proj - product(scaled[b], split(gram), NN)
        scaled.append(split(product(split(proj), split(fac_ref[c]), NT)))
        lane = slice(c * kb, (c + 1) * kb)
        high[:, lane], low[:, lane] = scaled[c]

    left = (high[...], low[...])
    out_copies = []
    for part, (start, width) in enumerate(spans):
        for copy in copies[part]:
            copy.wait()
        for at in range(0, width, 256):
            size = min(256, width - at)
            here = slice(start + at, start + at + size)
            right = jnp.concatenate(
                [vecs[part][:, b, :, at : at + size].reshape(kb, size) for b in range(nblk)],
                axis=0,
            )
            out[:, here] = eig_ref[:, here] - product(left, split(right), NN)
            if at + 256 >= width or at % 1024 == 768:
                first = at // 1024 * 1024
                lane = pl.ds(start + first, at + size - first)
                out_copies.append(
                    pltpu.make_async_copy(
                        out.at[:, lane], out_ref.at[:, lane], out_sems.at[len(out_copies)]
                    )
                )
                out_copies[-1].start()
    for copy in out_copies:
        copy.wait()


def update(order, info, sums, rest, factors, eig, parts):
    rows, cols = eig.shape
    nblk, kb, _ = factors.shape
    _, _, share, _ = parts[0][0].shape
    owners = kb // share
    vmem = pl.BlockSpec(memory_space=pltpu.VMEM)
    smem = pl.BlockSpec(memory_space=pltpu.SMEM)
    hbm = pl.BlockSpec(memory_space=pl.ANY)
    return pl.pallas_call(
        update_kernel,
        out_shape=jax.ShapeDtypeStruct(eig.shape, F32),
        in_specs=[smem] * 2 + [vmem] * 4 + [hbm] * 8,
        out_specs=hbm,
        scratch_shapes=[
            pltpu.VMEM((owners, nblk, share, parts[0][0].shape[3]), F32),
            pltpu.VMEM((owners, nblk, share, parts[1][0].shape[3]), F32),
            pltpu.VMEM((rows, cols), F32),
            pltpu.VMEM((rows, nblk * kb), BF16),
            pltpu.VMEM((rows, nblk * kb), BF16),
            pltpu.SemaphoreType.DMA((2, owners)),
            pltpu.SemaphoreType.DMA((8,)),
        ],
        compiler_params=pltpu.CompilerParams(vmem_limit_bytes=40 * 2**20),
        cost_estimate=pl.CostEstimate(
            flops=6 * rows * nblk * kb * cols,
            bytes_accessed=4 * cols * (2 * rows + nblk * kb),
            transcendentals=0,
        ),
        name="update",
    )(order, info, sums, rest, factors, eig, *parts[0], *parts[1])


def solution(mesh):
    placed = (P("pcol", "prow"), P(None, "pcol", "prow"), P(None, "pcol", None))
    nprow, npcol = mesh.shape["prow"], mesh.shape["pcol"]
    nz = nprow // 2
    orders = np.array([[arrival_order(route) for route in routes] for routes in ROUTES], np.int32)
    in_chip = [[2 * z, 2 * z + 1] for z in range(nz)]

    def send(x, masks):
        pairs = []
        for row in range(nprow):
            mask = masks[row % 2]
            pairs += [(row * npcol + at, row * npcol + (at ^ mask)) for at in range(npcol)]
        return lax.ppermute(x, ("prow", "pcol"), pairs)

    def gather_in_plane(own, part):
        steps = [(ROUTES[part][0][n], ROUTES[part][1][n]) for n in range(4)]
        held = own[None]
        held = jnp.concatenate([held, send(held, steps[0])], axis=0)
        held = jnp.concatenate([held, send(held, steps[1])], axis=0)
        third = send(held, steps[2])
        return held, third, send(held, steps[3]), send(third, steps[3])

    def along_z(x):
        groups = [list(range(core, nprow, 2)) for core in range(2)]
        return lax.all_to_all(x, "prow", 0, 0, axis_index_groups=groups)

    def sum_over_rows(keep, give):
        half, kb = keep.shape
        mine = keep + lax.ppermute(give, "prow", [(i, i ^ 1) for i in range(nprow)])
        part = jnp.sum(along_z(mine.reshape(nz, half // nz, kb)), axis=0)
        whole = along_z(jnp.broadcast_to(part, (nz,) + part.shape)).reshape(half, kb)
        pairs = [
            (row * npcol + at, row * npcol + (at ^ PARTNER))
            for row in range(1, nprow, 2)
            for at in range(npcol)
        ]
        other = lax.ppermute(whole, ("prow", "pcol"), pairs)
        sums = lax.all_gather(whole, "prow", axis=0, tiled=True, axis_index_groups=in_chip)
        sums, other = lax.optimization_barrier((sums, other))
        rest = lax.all_gather(other, "prow", axis=0, tiled=True, axis_index_groups=in_chip)
        return sums, rest[half:]

    def per_device(eig, house_vecs, wy_factor):
        nblk, _, kb = wy_factor.shape
        rows, cols = eig.shape
        data = (cols // 128 - 1) // 2 * 128
        at = lax.axis_index("pcol").astype(jnp.int32)
        core = lax.rem(lax.axis_index("prow"), 2).astype(jnp.int32)
        parity = jnp.bitwise_and(jnp.bitwise_xor(at >> 1, at >> 3), 1)
        info = jnp.stack([parity, core])
        order = jnp.bitwise_xor(at, jnp.where(core == 0, orders[:, 0], orders[:, 1]))
        own_a = jnp.concatenate([house_vecs[:, :, :data], wy_factor], axis=2)
        own_b = house_vecs[:, :, data:]
        part_a = gather_in_plane(own_a, 0)
        part_b = gather_in_plane(own_b, 1)
        early_a = collect(0, order, part_a[:3])
        early_b = collect(1, order, part_b[:3])
        order_a, early_b = lax.optimization_barrier((order, early_b))
        before, factors = inner_sums(0, data, order_a, info, eig, (early_a, part_a[3]))
        keep, give = inner_sums(
            1, cols - data, order, info, eig, (early_b, part_b[3]), before
        )
        sums, rest = sum_over_rows(keep, give)
        return update(order, info, sums, rest, factors, eig, (part_a, part_b))

    return jax.shard_map(
        per_device, mesh=mesh, in_specs=placed, out_specs=P("pcol", "prow"), check_vma=False
    )
```

```python
import jax
import jax.numpy as jnp
import numpy as np
from jax import lax
from jax.experimental import pallas as pl
from jax.experimental.pallas import tpu as pltpu
from jax.sharding import PartitionSpec as P

F32 = jnp.float32
BF16 = jnp.bfloat16
NT = (((1,), (1,)), ((), ()))
NN = (((1,), (0,)), ((), ()))
X_NEAR, X_WRAP, Y_NEAR, Y_WRAP = 4, 12, 1, 3
ROUTES = (
    ((X_NEAR, X_WRAP, Y_NEAR, Y_WRAP), (Y_NEAR, Y_WRAP, X_NEAR, X_WRAP)),
    ((X_WRAP, X_NEAR, Y_WRAP, Y_NEAR), (Y_WRAP, Y_NEAR, X_WRAP, X_NEAR)),
)
PARTNER = X_WRAP


def split(x):
    high = x.astype(BF16)
    low = (x - high.astype(F32)).astype(BF16)
    return high, low


def product(left, right, dims):
    rows = left[0].shape[0]
    both = lax.dot_general(
        jnp.concatenate(left, axis=0), right[0], dims, preferred_element_type=F32
    )
    cross = lax.dot_general(left[0], right[1], dims, preferred_element_type=F32)
    return both[:rows] + (both[rows:] + cross)


def exact(left, right, dims):
    return lax.dot_general(
        left, right, dims, precision=lax.Precision.HIGHEST, preferred_element_type=F32
    )


def pair_list(nblk):
    return [(b, c) for b in range(nblk) for c in range(b + 1, nblk)]


def block_row(block, rows, kb):
    return block * kb + (rows if block > 0 else 0)


def arrival_order(route):
    order = [0]
    for mask in route:
        order = order + [mask ^ at for at in order]
    return order


def owner_copies(order_ref, part, bufs, into, sems):
    copies = []
    for k, buf in enumerate(bufs):
        for i in range(buf.shape[0]):
            slot = k * buf.shape[0] + i
            copies.append(
                pltpu.make_async_copy(
                    buf.at[i], into.at[order_ref[part, slot]], sems.at[part, slot]
                )
            )
    return copies


def collect_kernel(part, order_ref, *refs):
    bufs, out_ref, sems = refs[:-2], refs[-2], refs[-1]
    copies = owner_copies(order_ref, part, bufs, out_ref, sems)
    for copy in copies:
        copy.start()
    for copy in copies:
        copy.wait()


def collect(part, order, bufs):
    _, nblk, share, width = bufs[0].shape
    owners = order.shape[1]
    return pl.pallas_call(
        lambda *refs: collect_kernel(part, *refs),
        out_shape=jax.ShapeDtypeStruct((owners, nblk, share, width), F32),
        in_specs=[pl.BlockSpec(memory_space=pltpu.SMEM)]
        + [pl.BlockSpec(memory_space=pl.ANY)] * len(bufs),
        out_specs=pl.BlockSpec(memory_space=pltpu.VMEM),
        scratch_shapes=[pltpu.SemaphoreType.DMA((2, owners))],
        compiler_params=pltpu.CompilerParams(vmem_limit_bytes=8 * 2**20),
        cost_estimate=pl.CostEstimate(
            flops=0, bytes_accessed=8 * owners * nblk * share * width, transcendentals=0
        ),
        name="collect",
    )(order, *bufs)


def inner_kernel(part, data, order_ref, info_ref, eig_ref, *refs):
    first = part == 0
    early_ref, late_ref, refs = refs[0], refs[1], refs[2:]
    if first:
        sum_ref, fac_ref, vecs, high, low = refs
    else:
        before_ref, keep_ref, give_ref, vecs, high, low, sum_ref = refs
    rows, cols = eig_ref.shape
    owners, nblk, share, _ = vecs.shape
    kb = owners * share
    start = 0 if first else cols - data

    count = late_ref.shape[0]
    for i in range(owners - count):
        owner = order_ref[part, i]
        vecs[owner] = early_ref[owner]
    for i in range(count):
        vecs[order_ref[part, owners - count + i]] = late_ref[i]

    eig_rows = slice(kb, kb + rows)
    high[eig_rows], low[eig_rows] = split(eig_ref[:, start : start + data])
    block = []
    for b in range(nblk):
        at = block_row(b, rows, kb)
        block.append(slice(at, at + kb))
        for owner in range(0, owners, 2):
            two = vecs[owner : owner + 2, b, :, :data].reshape(2 * share, data)
            here = slice(at + owner * share, at + (owner + 2) * share)
            high[here], low[here] = split(two)
    if first:
        for b in range(nblk):
            fac_ref[b] = vecs[:, b, :, data:].reshape(kb, kb)

    def inner(left, right):
        return product((high[left], low[left]), (high[right], low[right]), NT)

    def add(at, term):
        here = slice(at, at + term.shape[0])
        sum_ref[here] = term if first else before_ref[here] + term

    below = nblk * rows
    add(0, inner(eig_rows, block[0]))

    @pl.when(info_ref[0] == 0)
    def _():
        left = slice(0, kb + rows)
        out = inner(left, block[1])
        add(below, out[:kb])
        add(rows, out[kb:])
        out = inner(left, slice(block[2].start, block[3].stop))
        for c in (2, 3):
            lane = slice((c - 2) * kb, (c - 1) * kb)
            add(below + (c - 1) * kb, out[:kb, lane])
            add(c * rows, out[kb:, lane])

    @pl.when(info_ref[0] == 1)
    def _():
        add(rows, inner(eig_rows, block[1]))
        out = inner(slice(kb, block[2].stop), slice(block[2].start, block[3].stop))
        add(2 * rows, out[:rows, :kb])
        add(3 * rows, out[:rows, kb:])
        add(below, out[rows : rows + kb, :kb])
        add(below + kb, out[rows : rows + kb, kb:])
        add(below + 2 * kb, out[rows + kb :, kb:])

    if not first:
        half = keep_ref.shape[0]
        core = info_ref[1]
        keep_ref[...] = sum_ref[pl.ds(pl.multiple_of(core * half, 8), half)]
        give_ref[...] = sum_ref[pl.ds(pl.multiple_of((1 - core) * half, 8), half)]


def inner_sums(part, data, order, info, eig, bufs, before=None):
    rows, _ = eig.shape
    _, nblk, share, width = bufs[-1].shape
    owners = order.shape[1]
    kb = owners * share
    depth = rows + nblk * kb
    count = nblk * rows + len(pair_list(nblk)) // 2 * kb
    vmem = pl.BlockSpec(memory_space=pltpu.VMEM)
    smem = pl.BlockSpec(memory_space=pltpu.SMEM)
    sums = jax.ShapeDtypeStruct((count, kb), F32)
    scratch = [pltpu.VMEM((owners, nblk, share, width), F32)]
    scratch += [pltpu.VMEM((depth, data), BF16)] * 2
    if part == 0:
        outs = [sums, jax.ShapeDtypeStruct((nblk, kb, kb), F32)]
    else:
        outs = [jax.ShapeDtypeStruct((count // 2, kb), F32)] * 2
        scratch.append(pltpu.VMEM((count, kb), F32))
    return pl.pallas_call(
        lambda *refs: inner_kernel(part, data, *refs),
        out_shape=outs,
        in_specs=[smem, smem] + [vmem] * (1 + len(bufs) + part),
        out_specs=[vmem] * len(outs),
        scratch_shapes=scratch,
        compiler_params=pltpu.CompilerParams(vmem_limit_bytes=24 * 2**20),
        cost_estimate=pl.CostEstimate(
            flops=6 * data * kb * count, bytes_accessed=4 * data * depth, transcendentals=0
        ),
        name="inner_sums",
    )(order, info, eig, *bufs, *([before] if part == 1 else []))


def update_kernel(order_ref, info_ref, sum_ref, rest_ref, fac_ref, eig_ref, *refs):
    bufs = (refs[0:4], refs[4:8])
    out_ref, vecs, out, high, low, sems, out_sems = refs[8], refs[9:11], *refs[11:]
    rows, cols = eig_ref.shape
    nblk, kb, _ = fac_ref.shape
    below = nblk * rows
    pairs = pair_list(nblk)
    parity = info_ref[0]
    width_b = vecs[1].shape[3]
    spans = ((0, cols - width_b), (cols - width_b, width_b))

    copies = [owner_copies(order_ref, part, bufs[part], vecs[part], sems) for part in range(2)]
    for copy in copies[0] + copies[1]:
        copy.start()

    scaled = []
    for c in range(nblk):
        proj = sum_ref[c * rows : (c + 1) * rows]
        for b in range(c):
            index = pairs.index((b, c))
            at = index % (len(pairs) // 2) * kb
            mine = sum_ref[below + at : below + at + kb]
            rest = rest_ref[at : at + kb]
            gram = jnp.where((parity == 0) == (index < len(pairs) // 2), mine, rest)
            proj = proj - product(scaled[b], split(gram), NN)
        scaled.append(split(product(split(proj), split(fac_ref[c]), NT)))
        lane = slice(c * kb, (c + 1) * kb)
        high[:, lane], low[:, lane] = scaled[c]

    left = (high[...], low[...])
    out_copies = []
    for part, (start, width) in enumerate(spans):
        for copy in copies[part]:
            copy.wait()
        for at in range(0, width, 256):
            size = min(256, width - at)
            here = slice(start + at, start + at + size)
            right = jnp.concatenate(
                [vecs[part][:, b, :, at : at + size].reshape(kb, size) for b in range(nblk)],
                axis=0,
            )
            out[:, here] = eig_ref[:, here] - product(left, split(right), NN)
            if at + 256 >= width or at % 1024 == 768:
                first = at // 1024 * 1024
                lane = pl.ds(start + first, at + size - first)
                out_copies.append(
                    pltpu.make_async_copy(
                        out.at[:, lane], out_ref.at[:, lane], out_sems.at[len(out_copies)]
                    )
                )
                out_copies[-1].start()
    for copy in out_copies:
        copy.wait()


def update(order, info, sums, rest, factors, eig, parts):
    rows, cols = eig.shape
    nblk, kb, _ = factors.shape
    _, _, share, _ = parts[0][0].shape
    owners = kb // share
    vmem = pl.BlockSpec(memory_space=pltpu.VMEM)
    smem = pl.BlockSpec(memory_space=pltpu.SMEM)
    hbm = pl.BlockSpec(memory_space=pl.ANY)
    return pl.pallas_call(
        update_kernel,
        out_shape=jax.ShapeDtypeStruct(eig.shape, F32),
        in_specs=[smem] * 2 + [vmem] * 4 + [hbm] * 8,
        out_specs=hbm,
        scratch_shapes=[
            pltpu.VMEM((owners, nblk, share, parts[0][0].shape[3]), F32),
            pltpu.VMEM((owners, nblk, share, parts[1][0].shape[3]), F32),
            pltpu.VMEM((rows, cols), F32),
            pltpu.VMEM((rows, nblk * kb), BF16),
            pltpu.VMEM((rows, nblk * kb), BF16),
            pltpu.SemaphoreType.DMA((2, owners)),
            pltpu.SemaphoreType.DMA((8,)),
        ],
        compiler_params=pltpu.CompilerParams(vmem_limit_bytes=40 * 2**20),
        cost_estimate=pl.CostEstimate(
            flops=6 * rows * nblk * kb * cols,
            bytes_accessed=4 * cols * (2 * rows + nblk * kb),
            transcendentals=0,
        ),
        name="update",
    )(order, info, sums, rest, factors, eig, *parts[0], *parts[1])


def solution(mesh):
    placed = (P("pcol", "prow"), P(None, "pcol", "prow"), P(None, "pcol", None))
    nprow, npcol = mesh.shape["prow"], mesh.shape["pcol"]
    nz = nprow // 2
    orders = np.array([[arrival_order(route) for route in routes] for routes in ROUTES], np.int32)
    in_chip = [[2 * z, 2 * z + 1] for z in range(nz)]

    def send(x, masks):
        pairs = []
        for row in range(nprow):
            mask = masks[row % 2]
            pairs += [(row * npcol + at, row * npcol + (at ^ mask)) for at in range(npcol)]
        return lax.ppermute(x, ("prow", "pcol"), pairs)

    def gather_in_plane(own, part):
        steps = [(ROUTES[part][0][n], ROUTES[part][1][n]) for n in range(4)]
        held = own[None]
        held = jnp.concatenate([held, send(held, steps[0])], axis=0)
        held = jnp.concatenate([held, send(held, steps[1])], axis=0)
        third = send(held, steps[2])
        return held, third, send(held, steps[3]), send(third, steps[3])

    def along_z(x):
        groups = [list(range(core, nprow, 2)) for core in range(2)]
        return lax.all_to_all(x, "prow", 0, 0, axis_index_groups=groups)

    def sum_over_rows(keep, give):
        half, kb = keep.shape
        mine = keep + lax.ppermute(give, "prow", [(i, i ^ 1) for i in range(nprow)])
        part = jnp.sum(along_z(mine.reshape(nz, half // nz, kb)), axis=0)
        whole = along_z(jnp.broadcast_to(part, (nz,) + part.shape)).reshape(half, kb)
        pairs = [
            (row * npcol + at, row * npcol + (at ^ PARTNER))
            for row in range(1, nprow, 2)
            for at in range(npcol)
        ]
        other = lax.ppermute(whole, ("prow", "pcol"), pairs)
        sums = lax.all_gather(whole, "prow", axis=0, tiled=True, axis_index_groups=in_chip)
        sums, other = lax.optimization_barrier((sums, other))
        rest = lax.all_gather(other, "prow", axis=0, tiled=True, axis_index_groups=in_chip)
        return sums, rest[half:]

    def per_device(eig, house_vecs, wy_factor):
        nblk, _, kb = wy_factor.shape
        rows, cols = eig.shape
        data = (cols // 128 - 1) // 2 * 128
        at = lax.axis_index("pcol").astype(jnp.int32)
        core = lax.rem(lax.axis_index("prow"), 2).astype(jnp.int32)
        parity = jnp.bitwise_and(jnp.bitwise_xor(at >> 1, at >> 3), 1)
        info = jnp.stack([parity, core])
        order = jnp.bitwise_xor(at, jnp.where(core == 0, orders[:, 0], orders[:, 1]))
        own_a = jnp.concatenate([house_vecs[:, :, :data], wy_factor], axis=2)
        own_b = house_vecs[:, :, data:]
        part_a = gather_in_plane(own_a, 0)
        part_b = gather_in_plane(own_b, 1)
        early_a = collect(0, order, part_a[:3])
        early_b = collect(1, order, part_b[:3])
        order_a, early_b = lax.optimization_barrier((order, early_b))
        before, factors = inner_sums(0, data, order_a, info, eig, (early_a, part_a[3]))
        keep, give = inner_sums(
            1, cols - data, order, info, eig, (early_b, part_b[3]), before
        )
        sums, rest = sum_over_rows(keep, give)
        return update(order, info, sums, rest, factors, eig, (part_a, part_b))

    return jax.shard_map(
        per_device, mesh=mesh, in_specs=placed, out_specs=P("pcol", "prow"), check_vma=False
    )
```
